128 devices in a mesh: ep: 8 (over y, z_hi), dp: 16 (over z_lo, x, core).
Axes of the slice: x: 4, y: 4, z: 4 (z_hi: 2, z_lo: 2; z = z_hi * 2 + z_lo), core: 2. Of those that a mesh axis runs over, the one named last changes fastest.
Arguments:
- checkpoint: bfloat16 [16384, 2048], P('ep', 'dp'), may hold values from -6 to 6
- cotangent: bfloat16 [16384, 2048], P(('ep', 'dp')), may hold values from -6 to 6
- routes: int32 [16384, 2], P(('ep', 'dp')), may hold values from 0 to 7, all different within a row; in each aligned block of 128 rows (0 to 127, 128 to 255, ...) at most 64 rows name the same one
- gates: float32 [16384, 2], P(('ep', 'dp')), may hold values from 0.1 to 1
- w_gate: bfloat16 [8, 2048, 1024], P('ep'), may hold values from -0.125 to 0.125
- w_up: bfloat16 [8, 2048, 1024], P('ep'), may hold values from -0.125 to 0.125
- w_down: bfloat16 [8, 2048, 1024], P('ep'), may hold values from -0.1875 to 0.1875
Outputs:
- layer_out: bfloat16 [16384, 2048], P(('ep', 'dp'))
- grad_input: bfloat16 [16384, 2048], P(('ep', 'dp'))
- grad_gates: float32 [16384, 2], P(('ep', 'dp'))
- grad_w_gate: float32 [8, 2048, 1024], P('ep', 'dp')
- grad_w_up: float32 [8, 2048, 1024], P('ep', 'dp')
- grad_w_down: float32 [8, 2048, 1024], P('ep', 'dp')
The draws below stay inside these ranges and needn't reach their ends.
Inputs may be any that keep to these rules, and one draw needn't show every extreme that they name: `routes`: among the 128 rows of one device, no expert is named by more than 64 rows, and in every draw some expert is named by exactly 64 of them; a token names 2 different experts.
All inputs are finite; a program needn't handle non-finite values.
Results may differ from the reference program's by a relative error of at most 0.022.
Values may be sent and summed in bfloat16 or wider, within the bound.
No kernel may reach another device: no remote copies, remote signals or barrier semaphores. Data moves between devices by JAX's collectives and lax.ppermute only.
A program may use at most 128 MiB of HBM per device.

```python
import math
import jax
import jax.numpy as jnp
import numpy as np
from jax import lax

D = 2048
FF = 1024
TOP = 2
TOK_DEV = 128
EXPERTS = 8
CAP = 64
TOKENS = 16384
DEVICES = 128


def level_of(own_key, extent, split, smallest, largest):
    gain = 1.0
    for dim, blocks in split:
        heights = jax.random.uniform(jax.random.fold_in(jax.random.fold_in(own_key, 6), dim), (blocks,), jnp.float32, smallest / len(split), largest / len(split))
        gain = gain * jnp.repeat(jnp.exp(heights), extent[dim] // blocks).reshape((-1,) + (1,) * (len(extent) - 1 - dim))
    return gain


def routed_block(key, own, number, rows, amount, top, reach, lean):
    sequence = jax.random.permutation(key, amount)
    heavy_load, ordinary = load_shares(amount, rows * top, reach, lean, True), load_shares(amount, rows * top, reach, lean, False)
    places = jnp.arange(amount)

    def named(sizes, turn):
        used = int((sizes > 0).sum())
        fixed = max(1, used // 4)
        shifted = fixed + (places - fixed + turn * (used - fixed)) % max(1, amount - fixed)
        return jnp.zeros((amount,), jnp.int32).at[sequence[jnp.where(places < fixed, places, shifted)]].set(jnp.asarray(sizes, jnp.int32))

    sizes = jnp.where(number % 4 == 0, named(heavy_load, number // 4), named(ordinary, number - number // 4 - 1))
    mixed = jax.random.permutation(jax.random.fold_in(own, 3), amount)
    source_of, taker = mixed[0:amount // 2 * 2:2], mixed[1:amount // 2 * 2:2]
    room = jnp.minimum(sizes[source_of] - 1, reach - sizes[taker]) // 2
    room = jnp.where((source_of == sequence[0]) | (taker == sequence[0]) | (sizes[taker] == 0), 0, jnp.maximum(room, 0))
    shifted = jax.random.randint(jax.random.fold_in(own, 4), (amount // 2,), 0, 1 << 20) % (room + 1)
    sizes = sizes.at[source_of].add(-shifted).at[taker].add(shifted)
    items = jnp.searchsorted(jnp.cumsum(sizes), jnp.arange(rows * top), side="right").astype(jnp.int32)
    grid = items.reshape(top, rows).T
    grid = grid[jax.random.permutation(jax.random.fold_in(own, 1), rows)]
    turn = jax.random.randint(jax.random.fold_in(own, 2), (rows, 1), 0, top)
    return jnp.take_along_axis(grid, (jnp.arange(top)[None, :] + turn) % top, axis=1)


def load_shares(amount, total, most, lean, full):
    loads = [(1 << 20) // math.isqrt(standing ** lean) + 1 for standing in range(1, amount + 1)]
    largest = most if full else min(most, max(-(-total // amount), total * loads[0] // sum(loads)))
    least = 1 if total - largest >= amount - 1 else 0
    given, rest = [largest] + [least] * (amount - 1), total - largest - least * (amount - 1)
    while rest > 0:
        movable = [i for i in range(1, amount) if given[i] < largest] or [i for i in range(1, amount) if given[i] < most]
        pool, left = sum([loads[i] for i in movable]), rest
        for i in movable:
            addition = min(most - given[i], max(1, left * loads[i] // pool), rest)
            given[i] = given[i] + addition
            rest = rest - addition
    return np.array(given)


def noise(key, dims, scale, bound, shards=(), kind=jnp.bfloat16):
    loudness = level_of(key, dims, shards, -0.22, 0.18) if shards else 1.0
    values = jax.random.normal(key, dims, jnp.float32) * scale * loudness
    return jnp.minimum(jnp.maximum(values, -bound), bound).astype(kind)


def setup_inputs(seed: int = 0) -> dict:
    key_of = jax.random.split(jax.random.key(seed), 8)
    checkpoint = noise(key_of[0], (TOKENS, D), 1.0, 6.0, ((0, 8), (1, 16)))
    cotangent = noise(key_of[1], (TOKENS, D), 1.0, 6.0, ((0, 128),))
    routes_keys = jax.random.split(jax.random.fold_in(key_of[2], 1), TOKENS // TOK_DEV)
    routes_turns = jax.random.permutation(jax.random.fold_in(key_of[2], 3), TOKENS // TOK_DEV)
    routes = jax.vmap(lambda own, number: routed_block(jax.random.fold_in(key_of[2], 2), own, number, TOK_DEV, EXPERTS, TOP, CAP, 2))(routes_keys, routes_turns).reshape((TOKENS, TOP))
    gates = jnp.clip(jnp.exp(math.log(1.0) - 2.3025851 * jax.random.uniform(key_of[3], (TOKENS, TOP), jnp.float32) ** level_of(key_of[3], (TOKENS, TOP), ((0, 128),), -0.2, 0.2)), 0.1, 1.0)
    w_gate = noise(key_of[4], (EXPERTS, D, FF), D ** -0.5, 0.125, ((0, 8),))
    w_up = noise(key_of[5], (EXPERTS, D, FF), D ** -0.5, 0.125, ((0, 8),))
    w_down = noise(key_of[6], (EXPERTS, D, FF), FF ** -0.5, 0.1875, ((0, 8),))
    return {"checkpoint": checkpoint, "cotangent": cotangent, "routes": routes, "gates": gates, "w_gate": w_gate, "w_up": w_up, "w_down": w_down}


def reference(checkpoint, cotangent, routes, gates, w_gate, w_up, w_down):
    pair_count = TOKENS * TOP
    flat_routes = routes.reshape(-1).astype(jnp.int32)
    one_hot = (flat_routes[:, None] == jnp.arange(EXPERTS, dtype=jnp.int32)[None, :]).astype(jnp.int32)
    blocks = one_hot.reshape(DEVICES, TOK_DEV * TOP, EXPERTS)
    slot_index = (jnp.sum(jnp.cumsum(blocks, axis=1) * blocks, axis=2) - 1).reshape(-1)
    device_index = jnp.arange(pair_count, dtype=jnp.int32) // (TOK_DEV * TOP)
    position = (device_index * CAP + slot_index).astype(jnp.int32)
    source = jnp.full((EXPERTS, DEVICES * CAP), pair_count, jnp.int32)
    source = source.at[flat_routes, position].set(jnp.arange(pair_count, dtype=jnp.int32))
    x_padded = jnp.concatenate([checkpoint, jnp.zeros((1, D), jnp.bfloat16)], axis=0)
    grad_out = (gates[:, :, None] * cotangent[:, None, :].astype(jnp.float32)).astype(jnp.bfloat16)
    grad_padded = jnp.concatenate([grad_out.reshape(pair_count, D), jnp.zeros((1, D), jnp.bfloat16)], axis=0)

    def expert(operands):
        gate_w, up_w, down_w, rows_source = operands
        token_index = jnp.minimum(rows_source // TOP, TOKENS)
        x_rows = x_padded[token_index]
        d_rows = grad_padded[rows_source]
        pre_gate = jnp.dot(x_rows, gate_w, preferred_element_type=jnp.float32)
        pre_up = jnp.dot(x_rows, up_w, preferred_element_type=jnp.float32)
        activated = jax.nn.silu(pre_gate)
        hidden = (activated * pre_up).astype(jnp.bfloat16)
        outputs = jnp.dot(hidden, down_w.T, preferred_element_type=jnp.float32).astype(jnp.bfloat16)
        hidden_grad = jnp.dot(d_rows, down_w, preferred_element_type=jnp.float32)
        sigmoid_gate = jax.nn.sigmoid(pre_gate)
        gate_grad = (hidden_grad * pre_up * sigmoid_gate * (1.0 + pre_gate * (1.0 - sigmoid_gate))).astype(jnp.bfloat16)
        up_grad = (hidden_grad * activated).astype(jnp.bfloat16)
        input_part = (jnp.dot(gate_grad, gate_w.T, preferred_element_type=jnp.float32)
                      + jnp.dot(up_grad, up_w.T, preferred_element_type=jnp.float32)).astype(jnp.bfloat16)
        grad_gate_w = jnp.dot(x_rows.T, gate_grad, preferred_element_type=jnp.float32)
        grad_up_w = jnp.dot(x_rows.T, up_grad, preferred_element_type=jnp.float32)
        grad_down_w = jnp.dot(d_rows.T, hidden, preferred_element_type=jnp.float32)
        return outputs, input_part, grad_gate_w, grad_up_w, grad_down_w

    outputs_all, parts_all, grad_w_gate, grad_w_up, grad_w_down = lax.map(expert, (w_gate, w_up, w_down, source))
    expert_out = outputs_all[flat_routes, position].reshape(TOKENS, TOP, D).astype(jnp.float32)
    input_parts = parts_all[flat_routes, position].reshape(TOKENS, TOP, D).astype(jnp.float32)
    layer_out = jnp.sum(gates[:, :, None] * expert_out, axis=1).astype(jnp.bfloat16)
    grad_gates = jnp.sum(cotangent.astype(jnp.float32)[:, None, :] * expert_out, axis=-1)
    grad_input = jnp.sum(input_parts, axis=1).astype(jnp.bfloat16)
    return layer_out, grad_input, grad_gates, grad_w_gate, grad_w_up, grad_w_down
```

```python
import functools

import jax
import jax.numpy as jnp
from jax import lax
from jax.experimental import pallas as pl
from jax.experimental.pallas import tpu as pltpu
from jax.sharding import PartitionSpec as P

F32 = jnp.float32
BF16 = jnp.bfloat16
NT = (((1,), (1,)), ((), ()))
TN = (((0,), (0,)), ((), ()))
NN = (((1,), (0,)), ((), ()))
MIB = 1 << 20


def dot(a, b, dims=NN):
    return lax.dot_general(a, b, dims, preferred_element_type=F32)


def call(body, grid, in_specs, out_specs, out_shape, flops, moved, vmem=32):
    return pl.pallas_call(
        body,
        grid=grid,
        in_specs=in_specs,
        out_specs=out_specs,
        out_shape=out_shape,
        cost_estimate=pl.CostEstimate(flops=flops, bytes_accessed=moved, transcendentals=0),
        compiler_params=pltpu.CompilerParams(vmem_limit_bytes=vmem * MIB),
    )


def places(routes_ref, experts):
    tokens = routes_ref.shape[1]
    expert = lax.broadcasted_iota(jnp.int32, (experts, tokens), 0)
    first = (routes_ref[0:1, :] == expert).astype(F32)
    second = (routes_ref[1:2, :] == expert).astype(F32)
    chosen = first + second
    row = lax.broadcasted_iota(jnp.int32, (tokens, tokens), 0)
    col = lax.broadcasted_iota(jnp.int32, (tokens, tokens), 1)
    before = (row < col).astype(BF16)
    slot = dot(chosen.astype(BF16), before)
    return first, second, chosen, slot


def pick(mask, slot, e, cap):
    tokens = slot.shape[1]
    index = lax.broadcasted_iota(jnp.int32, (cap, tokens), 0).astype(F32)
    return jnp.where(index == slot[e : e + 1, :], mask[e : e + 1, :], 0.0)


def pack_kernel(experts, cap, scaled, routes_ref, gates_ref, rows_ref, out_ref):
    first, second, chosen, slot = places(routes_ref, experts)
    rows = rows_ref[...]
    weight = gates_ref[0:1, :] * first + gates_ref[1:2, :] * second
    for e in range(experts):
        sel = pick(chosen, slot, e, cap)
        picked = dot(sel.astype(BF16), rows)
        if scaled:
            picked = picked * jnp.sum(sel * weight[e : e + 1, :], axis=1, keepdims=True)
        out_ref[e * cap : (e + 1) * cap, :] = picked.astype(BF16)


def pack(routes, gates, rows, experts, cap, scaled):
    tokens, features = rows.shape
    whole = pl.BlockSpec(memory_space=pltpu.VMEM)
    return call(
        functools.partial(pack_kernel, experts, cap, scaled),
        (),
        [whole] * 3,
        whole,
        jax.ShapeDtypeStruct((experts * cap, features), BF16),
        2 * experts * cap * tokens * features,
        (experts * cap + tokens) * features * 2,
    )(routes, gates, rows)


def gather_sel(mask, slot, cap):
    experts = slot.shape[0]
    return jnp.concatenate([pick(mask, slot, e, cap) for e in range(experts)], axis=0)


def out_kernel(experts, cap, routes_ref, gates_ref, cot_ref, rows_ref, out_ref, grad_ref):
    first, second, _, slot = places(routes_ref, experts)
    rows = rows_ref[...]
    cot = cot_ref[...].astype(F32)
    gates = gates_ref[...]
    total = None
    columns = []
    for k, mask in enumerate((first, second)):
        sel = gather_sel(mask, slot, cap).astype(BF16)
        mine = dot(sel, rows, TN)
        columns.append(jnp.sum(cot * mine, axis=1, keepdims=True))
        term = gates[:, k : k + 1] * mine
        total = term if total is None else total + term
    out_ref[...] = total.astype(BF16)
    grad_ref[...] = jnp.concatenate(columns, axis=1)


def part_kernel(experts, cap, routes_ref, rows_ref, out_ref):
    _, _, chosen, slot = places(routes_ref, experts)
    sel = gather_sel(chosen, slot, cap).astype(BF16)
    out_ref[...] = dot(sel, rows_ref[...], TN).astype(BF16)


def hidden_grad_kernel(d_ref, w_ref, out_ref):
    out_ref[...] = dot(d_ref[...], w_ref[...])


def hidden_kernel(x_ref, wg_ref, wu_ref, hg_ref, h_ref, gg_ref, ug_ref):
    x = x_ref[...]
    pre_gate = dot(x, wg_ref[...])
    pre_up = dot(x, wu_ref[...])
    hidden_grad = hg_ref[...]
    s = 1.0 / (1.0 + jnp.exp(-pre_gate))
    silu = pre_gate * s
    h_ref[...] = (silu * pre_up).astype(BF16)
    gg_ref[...] = (hidden_grad * pre_up * s * (1.0 + pre_gate * (1.0 - s))).astype(BF16)
    ug_ref[...] = (hidden_grad * silu).astype(BF16)


def terms_kernel(ff, x_ref, d_ref, gg_ref, ug_ref, h_ref, out_ref):
    x = x_ref[...]
    d = d_ref[...]
    out_ref[:, 0:ff] = dot(x, gg_ref[...], TN).astype(BF16)
    out_ref[:, ff : 2 * ff] = dot(x, ug_ref[...], TN).astype(BF16)
    out_ref[:, 2 * ff : 3 * ff] = dot(d, h_ref[...], TN).astype(BF16)


def outputs_kernel(h_ref, w_ref, out_ref):
    out_ref[...] = dot(h_ref[...], w_ref[...], NT).astype(BF16)


def parts_kernel(gg_ref, ug_ref, wg_ref, wu_ref, out_ref):
    total = dot(gg_ref[...], wg_ref[...], NT) + dot(ug_ref[...], wu_ref[...], NT)
    out_ref[...] = total.astype(BF16)


def shards(checkpoint, cotangent, routes, gates, w_gate, w_up, w_down):
    tokens, features = cotangent.shape
    ep = lax.axis_size("ep")
    dp = lax.axis_size("dp")
    experts = ep * w_gate.shape[0]
    ff = w_gate.shape[2]
    cap = tokens * routes.shape[1] * 2 // experts
    rows = ep * cap
    block = 256
    whole = pl.BlockSpec(memory_space=pltpu.VMEM)
    w_gate, w_up, w_down = w_gate[0], w_up[0], w_down[0]
    routes_t = routes.T
    gates_t = gates.T
    mm = 2 * rows * features * ff

    slices = lax.all_to_all(
        checkpoint.reshape(dp, tokens, features // dp), "dp", split_axis=0, concat_axis=0, tiled=True
    )
    d_send = pack(routes_t, gates_t, cotangent, experts, cap, True)
    d_rows = lax.all_to_all(
        d_send.reshape(ep, cap, features), "ep", split_axis=0, concat_axis=0, tiled=True
    ).reshape(rows, features)
    inputs = jnp.transpose(slices, (1, 0, 2)).reshape(tokens, features)
    x_send = pack(routes_t, gates_t, inputs, experts, cap, False)
    x_rows = lax.all_to_all(
        x_send.reshape(ep, cap, features), "ep", split_axis=0, concat_axis=0, tiled=True
    ).reshape(rows, features)

    full_rows = pl.BlockSpec((rows, features), lambda i: (0, 0))
    full_hidden = pl.BlockSpec((rows, ff), lambda i: (0, 0))
    w_cols = pl.BlockSpec((features, block), lambda i: (0, i))
    w_rows = pl.BlockSpec((block, ff), lambda i: (i, 0))
    r_cols = pl.BlockSpec((rows, block), lambda i: (0, i))

    hidden_grad = call(
        hidden_grad_kernel,
        (ff // block,),
        [full_rows, w_cols],
        r_cols,
        jax.ShapeDtypeStruct((rows, ff), F32),
        mm,
        10 * MIB,
    )(d_rows, w_down)
    hidden, gate_grad, up_grad = call(
        hidden_kernel,
        (ff // block,),
        [full_rows, w_cols, w_cols, r_cols],
        [r_cols] * 3,
        [jax.ShapeDtypeStruct((rows, ff), BF16)] * 3,
        2 * mm,
        16 * MIB,
    )(x_rows, w_gate, w_up, hidden_grad)
    terms = call(
        functools.partial(terms_kernel, ff),
        (features // block,),
        [r_cols, r_cols, full_hidden, full_hidden, full_hidden],
        pl.BlockSpec((block, 3 * ff), lambda i: (i, 0)),
        jax.ShapeDtypeStruct((features, 3 * ff), BF16),
        3 * mm,
        19 * MIB,
    )(x_rows, d_rows, gate_grad, up_grad, hidden)
    summed = lax.psum_scatter(terms, "dp", scatter_dimension=0, tiled=True)
    outputs = call(
        outputs_kernel,
        (features // block,),
        [full_hidden, w_rows],
        r_cols,
        jax.ShapeDtypeStruct((rows, features), BF16),
        mm,
        7 * MIB,
    )(hidden, w_down)
    returned_out = lax.all_to_all(
        outputs.reshape(ep, cap, features), "ep", split_axis=0, concat_axis=0, tiled=True
    ).reshape(rows, features)
    parts = call(
        parts_kernel,
        (features // block,),
        [full_hidden, full_hidden, w_rows, w_rows],
        r_cols,
        jax.ShapeDtypeStruct((rows, features), BF16),
        2 * mm,
        12 * MIB,
    )(gate_grad, up_grad, w_gate, w_up)
    returned_part = lax.all_to_all(
        parts.reshape(ep, cap, features), "ep", split_axis=0, concat_axis=0, tiled=True
    ).reshape(rows, features)
    layer_out, grad_gates = call(
        functools.partial(out_kernel, experts, cap),
        (),
        [whole] * 4,
        [whole] * 2,
        [
            jax.ShapeDtypeStruct((tokens, features), BF16),
            jax.ShapeDtypeStruct((tokens, 2), F32),
        ],
        4 * rows * tokens * features,
        3 * MIB,
    )(routes_t, gates, cotangent, returned_out)
    grad_input = call(
        functools.partial(part_kernel, experts, cap),
        (),
        [whole] * 2,
        whole,
        jax.ShapeDtypeStruct((tokens, features), BF16),
        2 * rows * tokens * features,
        3 * MIB,
    )(routes_t, returned_part)
    grads = [summed[None, :, i * ff : (i + 1) * ff].astype(F32) for i in range(3)]
    return (layer_out, grad_input, grad_gates, *grads)


def solution(mesh):
    tok = P(("ep", "dp"), None)
    weight = P("ep", None, None)
    grad = P("ep", "dp", None)
    return jax.shard_map(
        shards,
        mesh=mesh,
        in_specs=(P("ep", "dp"), tok, tok, tok, weight, weight, weight),
        out_specs=(tok, tok, tok, grad, grad, grad),
        check_vma=False,
    )
```

```python
import functools

import jax
import jax.numpy as jnp
from jax import lax
from jax.experimental import pallas as pl
from jax.experimental.pallas import tpu as pltpu
from jax.sharding import PartitionSpec as P

F32 = jnp.float32
BF16 = jnp.bfloat16
NT = (((1,), (1,)), ((), ()))
TN = (((0,), (0,)), ((), ()))
NN = (((1,), (0,)), ((), ()))
MIB = 1 << 20

Y, Z, L, X, C = 4, 2, 2, 4, 2
EP_SWAP = [(i, i ^ 1) for i in range(Y * Z)]
DP_SWAP_L = [(i, i ^ (X * C)) for i in range(L * X * C)]
DP_SWAP_C = [(i, i ^ 1) for i in range(L * X * C)]
VMEM = pl.BlockSpec(memory_space=pltpu.VMEM)
ANY = pl.BlockSpec(memory_space=pl.ANY)
SMEM = pl.BlockSpec(memory_space=pltpu.SMEM)


def y_shift(k):
    return [(y * Z + z, (y + k) % Y * Z + z) for y in range(Y) for z in range(Z)]


def x_shift(k):
    return [
        ((line * X + x) * C + c, (line * X + (x + k) % X) * C + c)
        for line in range(L)
        for x in range(X)
        for c in range(C)
    ]


def struct(*shape, dtype=BF16):
    return jax.ShapeDtypeStruct(shape, dtype)


def dot(a, b, dims=NN):
    return lax.dot_general(a, b, dims, preferred_element_type=F32)


def spec(shape, index=None):
    zeros = (0,) * len(shape)
    return pl.BlockSpec(shape, index or (lambda *_: zeros))


def call(body, out_shape, args, flops=0, in_specs=None, out_specs=None, vmem=32, scratch=()):
    in_specs = in_specs or [None] * len(args)
    out_specs = out_specs or [None] * len(out_shape)
    return pl.pallas_call(
        body,
        in_specs=[s or VMEM for s in in_specs],
        out_specs=[s or VMEM for s in out_specs],
        out_shape=out_shape,
        scratch_shapes=scratch,
        cost_estimate=pl.CostEstimate(
            flops=flops,
            bytes_accessed=sum(a.size * a.dtype.itemsize for a in args),
            transcendentals=0,
        ),
        compiler_params=pltpu.CompilerParams(vmem_limit_bytes=vmem * MIB),
    )(*args)


def streamed(body, out_shape, args, flops, scratch, in_count, out_count, in_specs=None):
    sems = [pltpu.SemaphoreType.DMA((in_count,)), pltpu.SemaphoreType.DMA((out_count,))]
    return call(
        body,
        out_shape,
        args,
        flops,
        in_specs=in_specs or [ANY] * len(args),
        out_specs=[ANY] * len(out_shape),
        vmem=56,
        scratch=[pltpu.VMEM(shape, dtype) for shape, dtype in scratch] + sems,
    )


def started(pairs, sems):
    copies = [pltpu.make_async_copy(a, b, sems.at[n]) for n, (a, b) in enumerate(pairs)]
    for copy in copies:
        copy.start()
    return copies


def places(code_ref, count):
    tokens = code_ref.shape[1]
    expert = lax.broadcasted_iota(jnp.int32, (count, tokens), 0)
    first = (code_ref[0:1, :] == expert).astype(F32)
    second = (code_ref[1:2, :] == expert).astype(F32)
    row = lax.broadcasted_iota(jnp.int32, (tokens, tokens), 0)
    col = lax.broadcasted_iota(jnp.int32, (tokens, tokens), 1)
    before = (row < col).astype(BF16)
    slot = dot((first + second).astype(BF16), before)
    return first, second, slot


def pick(mask, slot, cap):
    count, tokens = slot.shape
    index = lax.broadcasted_iota(jnp.int32, (cap, tokens), 0).astype(F32)
    return jnp.concatenate(
        [jnp.where(index == slot[e : e + 1, :], mask[e : e + 1, :], 0.0) for e in range(count)], axis=0
    )


def pack_d_kernel(cap, code_ref, gates_ref, rows_ref, *out_refs):
    first, second, slot = places(code_ref, Y)
    sel = pick(first + second, slot, cap)
    weight = gates_ref[0:1, :] * first + gates_ref[1:2, :] * second
    scale = jnp.concatenate(
        [
            jnp.sum(sel[e * cap : (e + 1) * cap, :] * weight[e : e + 1, :], axis=1, keepdims=True)
            for e in range(Y)
        ],
        axis=0,
    )
    picked = (dot(sel.astype(BF16), rows_ref[...]) * scale).astype(BF16)
    for e, out_ref in enumerate(out_refs):
        out_ref[...] = picked[e * cap : (e + 1) * cap, :]


def pack_x_kernel(cap, routes_ref, slices_ref, *refs):
    first, second, slot = places(routes_ref, Y * Z)
    sel = pick(first + second, slot, cap).astype(BF16)
    out_ref = refs[-1]
    width = slices_ref.shape[2]
    for j in range(slices_ref.shape[0]):
        out_ref[:, j * width : (j + 1) * width] = dot(sel, slices_ref[j]).astype(BF16)


def hidden_grad_kernel(at_ref, *refs):
    *d_refs, w_ref, out_ref, rows_ref, d, w, out, ins, outs = refs
    cap = d_refs[0].shape[0]
    cuts = [slice(0, 512), slice(512, 1024)]
    pairs = [(r, d.at[pl.ds(pl.multiple_of(at_ref[n] * cap, cap), cap)]) for n, r in enumerate(d_refs)]
    copies = started(pairs + [(w_ref.at[:, c], w.at[:, c]) for c in cuts], ins)
    for copy in copies[: len(pairs)]:
        copy.wait()
    back = [pltpu.make_async_copy(d, rows_ref, outs.at[2])]
    back[0].start()
    for n, c in enumerate(cuts):
        copies[len(pairs) + n].wait()
        out[:, c] = dot(d[...], w[:, c])
        back.append(pltpu.make_async_copy(out.at[:, c], out_ref.at[:, c], outs.at[n]))
        back[-1].start()
    for copy in back:
        copy.wait()


def hidden_kernel(x_ref, wg_ref, wu_ref, hg_ref, out_ref, x, wg, wu, hg, out, ins, outs):
    cuts = [slice(0, 256), slice(256, 512), slice(512, 1024)]
    pairs = [(x_ref, x)]
    for c in cuts:
        pairs += [(a.at[:, c], b.at[:, c]) for a, b in ((wg_ref, wg), (wu_ref, wu), (hg_ref, hg))]
    copies = started(pairs, ins)
    copies[0].wait()
    back = []
    for n, c in enumerate(cuts):
        for copy in copies[1 + 3 * n : 4 + 3 * n]:
            copy.wait()
        pre_gate = dot(x[...], wg[:, c])
        pre_up = dot(x[...], wu[:, c])
        hidden_grad = hg[:, c]
        s = 0.5 * jnp.tanh(0.5 * pre_gate) + 0.5
        silu = pre_gate * s
        out[0, :, c] = (hidden_grad * pre_up * s * (1.0 + pre_gate * (1.0 - s))).astype(BF16)
        out[1, :, c] = (hidden_grad * silu).astype(BF16)
        out[2, :, c] = (silu * pre_up).astype(BF16)
        back.append(pltpu.make_async_copy(out.at[:, :, c], out_ref.at[:, :, c], outs.at[n]))
        back[-1].start()
    for copy in back:
        copy.wait()


def turn_kernel(start_ref, rows_ref, own_ref, other_ref):
    width = own_ref.shape[0] // (L * X)
    for n, out_ref in enumerate((own_ref, other_ref)):
        for j in range(L * X):
            begin = pl.multiple_of(start_ref[n * L * X + j], width)
            out_ref[j * width : (j + 1) * width, :] = rows_ref[:, pl.ds(begin, width)].T


def terms_kernel(n, xo_ref, xp_ref, do_ref, dp_ref, ho_ref, hp_ref, *refs):
    out_refs, (xo, xp, do, dp, ho, hp, out, ins, outs) = refs[1:6], refs[6:]
    size = xo.shape[0]
    rows = slice(n * size, (n + 1) * size)
    pairs = [
        (xo_ref.at[rows], xo),
        (ho_ref.at[0], ho.at[0]),
        (xp_ref.at[rows], xp),
        (hp_ref.at[0], hp.at[0]),
        (ho_ref.at[1], ho.at[1]),
        (hp_ref.at[1], hp.at[1]),
        (do_ref.at[rows], do),
        (ho_ref.at[2], ho.at[2]),
        (dp_ref.at[rows], dp),
        (hp_ref.at[2], hp.at[2]),
    ]
    copies = started(pairs, ins)
    back = []
    for i, (own, peer, ready) in enumerate(((xo, xp, copies[:4]), (xo, xp, copies[4:6]), (do, dp, copies[6:]))):
        for copy in ready:
            copy.wait()
        out[i] = (dot(own[...], ho[i]) + dot(peer[...], hp[i])).astype(BF16)
        begin = 0
        for r in out_refs:
            count = r.shape[1]
            back.append(pltpu.make_async_copy(out.at[i, begin : begin + count], r.at[i], outs.at[len(back)]))
            back[-1].start()
            begin += count
    for copy in back:
        copy.wait()


def near_kernel(up_ref, down_ref, own_up_ref, own_down_ref, *refs):
    to_up_ref, to_down_ref = refs[-2:]
    half = up_ref.shape[1]
    for own_ref, got_ref, out_ref, rows in (
        (own_up_ref, up_ref, to_up_ref, slice(0, half)),
        (own_down_ref, down_ref, to_down_ref, slice(half, 2 * half)),
    ):
        out_ref[...] = own_ref[...]
        out_ref[:, rows, :] = (own_ref[:, rows, :].astype(F32) + got_ref[...].astype(F32)).astype(BF16)


def line_kernel(own_ref, from_up_ref, from_down_ref, *refs):
    line_ref = refs[-3]
    for i in range(3):
        total = own_ref[i].astype(F32) + from_up_ref[i].astype(F32) + from_down_ref[i].astype(F32)
        line_ref[i] = total.astype(BF16)
    near_kernel(*refs[:4], *refs[-2:])


def sum_kernel(*refs):
    *in_refs, gate_ref, up_ref, down_ref = refs
    for i, out_ref in enumerate((gate_ref, up_ref, down_ref)):
        total = in_refs[0][i].astype(F32)
        for r in in_refs[1:]:
            total = total + r[i].astype(F32)
        out_ref[0] = total


def outputs_kernel(cap, hid_ref, wd_ref, wg_ref, wu_ref, out_ref, hid, wd, wg, wu, out, ins, outs):
    cuts = [slice(n * 512, (n + 1) * 512) for n in range(wd.shape[0] // 512)]
    pairs = [(hid_ref.at[2], hid.at[2]), (wd_ref.at[cuts[0]], wd.at[cuts[0]])]
    pairs += [(hid_ref.at[0:2], hid.at[0:2])]
    pairs += [(wg_ref.at[cuts[0]], wg.at[cuts[0]]), (wu_ref.at[cuts[0]], wu.at[cuts[0]])]
    for c in cuts[1:]:
        pairs += [(a.at[c], b.at[c]) for a, b in ((wd_ref, wd), (wg_ref, wg), (wu_ref, wu))]
    copies = started(pairs, ins)
    back = []
    for n, c in enumerate(cuts):
        first = copies[:2] if n == 0 else copies[3 * n + 2 : 3 * n + 3]
        then = copies[2:5] if n == 0 else copies[3 * n + 3 : 3 * n + 5]
        for copy in first:
            copy.wait()
        term = dot(hid[2], wd[c], NT).astype(BF16)
        for s in range(Y * Z):
            out[s, 0, :, c] = term[s * cap : (s + 1) * cap, :]
        for copy in then:
            copy.wait()
        term = (dot(hid[0], wg[c], NT) + dot(hid[1], wu[c], NT)).astype(BF16)
        for s in range(Y * Z):
            out[s, 1, :, c] = term[s * cap : (s + 1) * cap, :]
        back.append(pltpu.make_async_copy(out.at[:, :, :, c], out_ref.at[:, :, :, c], outs.at[n]))
        back[-1].start()
    for copy in back:
        copy.wait()


def combine_kernel(routes_ref, gates_ref, cot_ref, rows_ref, out_ref, part_ref, grad_ref):
    cap = rows_ref.shape[2]
    first, second, slot = places(routes_ref, Y * Z)
    outs = jnp.concatenate([rows_ref[e, 0] for e in range(Y * Z)], axis=0)
    parts = jnp.concatenate([rows_ref[e, 1] for e in range(Y * Z)], axis=0)
    cot = cot_ref[...].astype(F32)
    total, columns = None, []
    for k, mask in enumerate((first, second)):
        mine = dot(pick(mask, slot, cap).astype(BF16), outs, TN)
        columns.append(jnp.sum(cot * mine, axis=1, keepdims=True))
        term = gates_ref[:, k : k + 1] * mine
        total = term if total is None else total + term
    out_ref[...] = total.astype(BF16)
    part_ref[...] = dot(pick(first + second, slot, cap).astype(BF16), parts, TN).astype(BF16)
    grad_ref[...] = jnp.concatenate(columns, axis=1)


def shards(checkpoint, cotangent, routes, gates, w_gate, w_up, w_down):
    tokens, features = cotangent.shape
    dp = lax.axis_size("dp")
    ff = w_gate.shape[2]
    experts = Y * Z
    cap = tokens * routes.shape[1] * 2 // experts
    rows = experts * cap
    w_gate, w_up, w_down = w_gate[0], w_up[0], w_down[0]
    mm = 2 * rows * features * ff
    y, z = lax.axis_index("ep") // Z, lax.axis_index("ep") % Z
    mine = lax.axis_index("dp")
    line, x_at, core = mine // (X * C), mine // C % X, mine % C
    step = jnp.arange(C * L * X, dtype=jnp.int32)
    block_at = (line ^ (1 - step // X % L)) * X + (x_at + step) % X
    start = (block_at * C + (core ^ (step // (L * X)))).astype(jnp.int32) * (features // dp)
    piece_at = ((y - step[: Y * Z]) % Y * Z + (z ^ (step[: Y * Z] // Y))).astype(jnp.int32)

    routes_t, gates_t = routes.T, gates.T
    slices = lax.all_to_all(
        checkpoint.reshape(dp, tokens, features // dp), "dp", split_axis=0, concat_axis=0, tiled=True
    )
    info = lax.ppermute(jnp.concatenate([routes_t.astype(F32), gates_t], axis=0), "ep", EP_SWAP)
    cot_p = lax.ppermute(cotangent, "ep", EP_SWAP)

    def codes(route):
        return jnp.where(route % Z == z, (route // Z - y) % Y, -1)

    code_o, code_p = codes(routes_t), codes(info[:2].astype(jnp.int32))

    def pack_d(code, gate, source):
        return call(
            functools.partial(pack_d_kernel, cap),
            [struct(cap, features)] * Y,
            [code, gate, source],
            2 * Y * cap * tokens * features,
            vmem=16,
        )

    def to_experts(packed):
        return [packed[0]] + [lax.ppermute(packed[k], "ep", y_shift(k)) for k in range(1, Y)]

    d_own = to_experts(pack_d(code_o, gates_t, cotangent))
    (x_send,) = call(
        functools.partial(pack_x_kernel, cap),
        [struct(rows, features)],
        [routes_t, slices, cot_p, info, *d_own],
        2 * rows * tokens * features,
        in_specs=[None, None] + [ANY] * (2 + Y),
        vmem=16,
    )
    x_rows = lax.all_to_all(
        x_send.reshape(experts, cap, features), "ep", split_axis=0, concat_axis=0, tiled=True
    ).reshape(rows, features)
    d_pieces = d_own + to_experts(pack_d(code_p, info[2:], cot_p))

    hidden_grad, d_rows = streamed(
        hidden_grad_kernel,
        [struct(rows, ff, dtype=F32), struct(rows, features)],
        [piece_at, *d_pieces, w_down],
        mm,
        [((rows, features), BF16), ((features, ff), BF16), ((rows, ff), F32)],
        experts + 2,
        3,
        in_specs=[SMEM] + [ANY] * (experts + 1),
    )

    def turn(array):
        own, other = call(
            turn_kernel,
            [struct(features // C, rows)] * 2,
            [start, array],
            in_specs=[SMEM, None],
            vmem=24,
        )
        return own, lax.ppermute(other, "dp", DP_SWAP_C)

    d_turned = turn(d_rows)
    weight = ((features, ff), BF16)
    (hid,) = streamed(
        hidden_kernel,
        [struct(3, rows, ff)],
        [x_rows, w_gate, w_up, hidden_grad],
        2 * mm,
        [((rows, features), BF16), weight, weight, ((rows, ff), F32), ((3, rows, ff), BF16)],
        10,
        3,
    )
    hid_peer = lax.ppermute(hid, "dp", DP_SWAP_C)
    x_turned = turn(x_rows)
    (outs,) = streamed(
        functools.partial(outputs_kernel, cap),
        [struct(experts, 2, cap, features)],
        [hid, w_down, w_gate, w_up],
        3 * mm,
        [((3, rows, ff), BF16), weight, weight, weight, ((experts, 2, cap, features), BF16)],
        14,
        4,
    )
    back = lax.all_to_all(outs, "ep", split_axis=0, concat_axis=0, tiled=True)

    half = tokens // 2
    sizes = (tokens, tokens, half, half, tokens)

    def terms_of(n, after):
        size = X * tokens
        return streamed(
            functools.partial(terms_kernel, n),
            [struct(3, count, ff) for count in sizes],
            [*x_turned, *d_turned, hid, hid_peer, after],
            3 * mm // 2,
            [((size, rows), BF16)] * 4 + [((3, rows, ff), BF16)] * 2 + [((3, size, ff), BF16)],
            10,
            15,
        )

    def small(body, count, arrays, after=()):
        return call(
            body,
            [struct(3, tokens, ff)] * count,
            [*arrays, *after],
            in_specs=[None] * len(arrays) + [ANY] * len(after),
            vmem=24,
        )

    def shift(array, k):
        return lax.ppermute(array, "dp", x_shift(k))

    there = terms_of(0, outs)
    there_up, there_down = shift(there[2], 1), shift(there[3], -1)
    here = terms_of(1, there[0])
    here_up, here_down = shift(here[2], 1), shift(here[3], -1)
    to_up, to_down = small(near_kernel, 2, (there_up, there_down, there[1], there[4]), here[:1])
    there_up, there_down = shift(to_up, 1), shift(to_down, -1)
    other, to_up, to_down = small(
        line_kernel, 3, (there[0], there_up, there_down, here_up, here_down, here[1], here[4])
    )
    other = lax.ppermute(other, "dp", DP_SWAP_L)
    here_up, here_down = shift(to_up, 1), shift(to_down, -1)
    grads = call(
        sum_kernel, [struct(1, tokens, ff, dtype=F32)] * 3, [here[0], here_up, here_down, other], vmem=24
    )
    layer_out, grad_input, grad_gates = call(
        combine_kernel,
        [struct(tokens, features), struct(tokens, features), struct(tokens, 2, dtype=F32)],
        [routes_t, gates, cotangent, back],
        6 * rows * tokens * features,
        vmem=32,
    )
    return (layer_out, grad_input, grad_gates, *grads)


def solution(mesh):
    tok = P(("ep", "dp"), None)
    weight = P("ep", None, None)
    grad = P("ep", "dp", None)
    return jax.shard_map(
        shards,
        mesh=mesh,
        in_specs=(P("ep", "dp"), tok, tok, tok, weight, weight, weight),
        out_specs=(tok, tok, tok, grad, grad, grad),
        check_vma=False,
    )
```

```python
import functools

import jax
import jax.numpy as jnp
from jax import lax
from jax.experimental import pallas as pl
from jax.experimental.pallas import tpu as pltpu
from jax.sharding import PartitionSpec as P

F32 = jnp.float32
BF16 = jnp.bfloat16
NT = (((1,), (1,)), ((), ()))
TN = (((0,), (0,)), ((), ()))
NN = (((1,), (0,)), ((), ()))
MIB = 1 << 20

Y, Z, L, X, C = 4, 2, 2, 4, 2
EP_SWAP = [(i, i ^ 1) for i in range(Y * Z)]
DP_SWAP_L = [(i, i ^ (X * C)) for i in range(L * X * C)]
DP_SWAP_C = [(i, i ^ 1) for i in range(L * X * C)]
VMEM = pl.BlockSpec(memory_space=pltpu.VMEM)
ANY = pl.BlockSpec(memory_space=pl.ANY)
SMEM = pl.BlockSpec(memory_space=pltpu.SMEM)


def y_shift(k):
    return [(y * Z + z, (y + k) % Y * Z + z) for y in range(Y) for z in range(Z)]


def x_shift(k):
    return [
        ((line * X + x) * C + c, (line * X + (x + k) % X) * C + c)
        for line in range(L)
        for x in range(X)
        for c in range(C)
    ]


def struct(*shape, dtype=BF16):
    return jax.ShapeDtypeStruct(shape, dtype)


def dot(a, b, dims=NN):
    return lax.dot_general(a, b, dims, preferred_element_type=F32)


def spec(shape, index=None):
    zeros = (0,) * len(shape)
    return pl.BlockSpec(shape, index or (lambda *_: zeros))


def call(body, out_shape, args, flops=0, in_specs=None, out_specs=None, vmem=32, scratch=(), blocks=False):
    in_specs = in_specs or [None] * len(args)
    out_specs = out_specs or [None] * len(out_shape)

    def whole(array):
        return spec(array.shape) if blocks else VMEM

    return pl.pallas_call(
        body,
        grid=(1,) if blocks else (),
        in_specs=[s or whole(a) for s, a in zip(in_specs, args, strict=True)],
        out_specs=[s or whole(a) for s, a in zip(out_specs, out_shape, strict=True)],
        out_shape=out_shape,
        scratch_shapes=scratch,
        cost_estimate=pl.CostEstimate(
            flops=flops,
            bytes_accessed=sum(a.size * a.dtype.itemsize for a in args),
            transcendentals=0,
        ),
        compiler_params=pltpu.CompilerParams(vmem_limit_bytes=vmem * MIB),
    )(*args)


def streamed(body, out_shape, args, flops, scratch, in_count, out_count, in_specs=None):
    sems = [pltpu.SemaphoreType.DMA((in_count,)), pltpu.SemaphoreType.DMA((out_count,))]
    return call(
        body,
        out_shape,
        args,
        flops,
        in_specs=in_specs or [ANY] * len(args),
        out_specs=[ANY] * len(out_shape),
        vmem=56,
        scratch=[pltpu.VMEM(shape, dtype) for shape, dtype in scratch] + sems,
    )


def started(pairs, sems):
    copies = [pltpu.make_async_copy(a, b, sems.at[n]) for n, (a, b) in enumerate(pairs)]
    for copy in copies:
        copy.start()
    return copies


def places(code_ref, count):
    tokens = code_ref.shape[1]
    expert = lax.broadcasted_iota(jnp.int32, (count, tokens), 0)
    first = (code_ref[0:1, :] == expert).astype(F32)
    second = (code_ref[1:2, :] == expert).astype(F32)
    row = lax.broadcasted_iota(jnp.int32, (tokens, tokens), 0)
    col = lax.broadcasted_iota(jnp.int32, (tokens, tokens), 1)
    before = (row < col).astype(BF16)
    slot = dot((first + second).astype(BF16), before)
    return first, second, slot


def pick(mask, slot, cap):
    count, tokens = slot.shape
    index = lax.broadcasted_iota(jnp.int32, (cap, tokens), 0).astype(F32)
    return jnp.concatenate(
        [jnp.where(index == slot[e : e + 1, :], mask[e : e + 1, :], 0.0) for e in range(count)], axis=0
    )


def codes(routes, at_ref):
    return jnp.where((routes & 1) == at_ref[1], ((routes >> 1) - at_ref[0]) & (Y - 1), -1)


def pack_d(cap, code_ref, gates, rows, out_refs):
    first, second, slot = places(code_ref, Y)
    sel = pick(first + second, slot, cap)
    weight = gates[0:1, :] * first + gates[1:2, :] * second
    scale = jnp.concatenate(
        [
            jnp.sum(sel[e * cap : (e + 1) * cap, :] * weight[e : e + 1, :], axis=1, keepdims=True)
            for e in range(Y)
        ],
        axis=0,
    )
    picked = (dot(sel.astype(BF16), rows) * scale).astype(BF16)
    for e, out_ref in enumerate(out_refs):
        out_ref[...] = picked[e * cap : (e + 1) * cap, :]


def own_kernel(cap, at_ref, routes_ref, gates_ref, cot_ref, ck_ref, code_ref, wide_ref, ck_out_ref, *out_refs):
    features = cot_ref.shape[1]
    wide_ref[:, 0:features] = cot_ref[...]
    ck_out_ref[...] = ck_ref[...]
    gates = gates_ref[...]
    pieces, rest = [routes_ref[...].astype(F32)], gates
    for _ in range(3):
        pieces.append(rest.astype(BF16).astype(F32))
        rest = rest - pieces[-1]
    tokens = gates.shape[1]
    columns = jnp.concatenate([*pieces, jnp.zeros((tokens - 8, tokens), F32)], axis=0)
    wide_ref[:, features:] = columns.T.astype(BF16)
    code_ref[...] = codes(routes_ref[...], at_ref)
    pack_d(cap, code_ref, gates, cot_ref[...], out_refs)


def copy_kernel(in_ref, _, out_ref):
    out_ref[...] = in_ref[...]


def partner_kernel(cap, at_ref, wide_ref, *refs):
    code_ref, *out_refs = refs[-1 - Y :]
    features = out_refs[0].shape[1]
    columns = wide_ref[:, features:].astype(F32).T
    code_ref[...] = codes(columns[0:2, :].astype(jnp.int32), at_ref)
    gates = columns[2:4, :] + columns[4:6, :] + columns[6:8, :]
    pack_d(cap, code_ref, gates, wide_ref[:, 0:features], out_refs)


def pack_x_kernel(cap, code_o_ref, code_p_ref, slices_o_ref, slices_p_ref, *refs):
    out_refs = refs[-Y:]
    width = slices_o_ref.shape[2]
    for n, (code_ref, slices_ref) in enumerate(((code_o_ref, slices_o_ref), (code_p_ref, slices_p_ref))):
        first, second, slot = places(code_ref, Y)
        sel = pick(first + second, slot, cap).astype(BF16)
        for j in range(slices_ref.shape[0]):
            picked = dot(sel, slices_ref[j]).astype(BF16)
            for k, out_ref in enumerate(out_refs):
                out_ref[n * cap : (n + 1) * cap, j * width : (j + 1) * width] = picked[k * cap : (k + 1) * cap, :]


def turn(rows, start_ref, own, other):
    width = own.shape[0] // (L * X)
    for n, out in enumerate((own, other)):
        for j in range(L * X):
            begin = pl.multiple_of(start_ref[n * L * X + j], width)
            out[j * width : (j + 1) * width, :] = rows[:, pl.ds(begin, width)].T


def hidden_grad_kernel(at_ref, start_ref, *refs):
    *d_refs, w_ref, out_ref, own_ref, other_ref, d, w, out, own, other, ins, outs = refs
    cap = d_refs[0].shape[0]
    cuts = [slice(0, 512), slice(512, 1024)]
    pairs = [(r, d.at[pl.ds(pl.multiple_of(at_ref[n] * cap, cap), cap)]) for n, r in enumerate(d_refs)]
    copies = started(pairs + [(w_ref.at[:, c], w.at[:, c]) for c in cuts], ins)
    for copy in copies[: len(pairs)]:
        copy.wait()
    turn(d, start_ref, own, other)
    back = [pltpu.make_async_copy(a, b, outs.at[2 + n]) for n, (a, b) in enumerate(((own, own_ref), (other, other_ref)))]
    for copy in back:
        copy.start()
    for n, c in enumerate(cuts):
        copies[len(pairs) + n].wait()
        out[:, c] = dot(d[...], w[:, c])
        back.append(pltpu.make_async_copy(out.at[:, c], out_ref.at[:, c], outs.at[n]))
        back[-1].start()
    for copy in back:
        copy.wait()


def hidden_kernel(at_ref, start_ref, *refs):
    x_refs, refs = refs[:Y], refs[Y:]
    wg_ref, wu_ref, hg_ref, out_ref, own_ref, other_ref, x, wg, wu, hg, out, own, other, ins, outs = refs
    cuts = [slice(0, 256), slice(256, 512), slice(512, 1024)]
    cap = x_refs[0].shape[0] // 2
    pairs = [
        (r.at[n * cap : (n + 1) * cap], x.at[pl.ds(pl.multiple_of(at_ref[n * Y + k] * cap, cap), cap)])
        for k, r in enumerate(x_refs)
        for n in range(2)
    ]
    count = len(pairs)
    for c in cuts:
        pairs += [(a.at[:, c], b.at[:, c]) for a, b in ((wg_ref, wg), (wu_ref, wu), (hg_ref, hg))]
    copies = started(pairs, ins)
    for copy in copies[:count]:
        copy.wait()
    back = []
    for n, c in enumerate(cuts):
        for copy in copies[count + 3 * n : count + 3 * n + 3]:
            copy.wait()
        pre_gate = dot(x[...], wg[:, c])
        pre_up = dot(x[...], wu[:, c])
        if n == 0:
            turn(x, start_ref, own, other)
            back += [pltpu.make_async_copy(own, own_ref, outs.at[3]), pltpu.make_async_copy(other, other_ref, outs.at[4])]
            for copy in back:
                copy.start()
        hidden_grad = hg[:, c]
        s = 0.5 * jnp.tanh(0.5 * pre_gate) + 0.5
        silu = pre_gate * s
        out[0, :, c] = (hidden_grad * pre_up * s * (1.0 + pre_gate * (1.0 - s))).astype(BF16)
        out[1, :, c] = (hidden_grad * silu).astype(BF16)
        out[2, :, c] = (silu * pre_up).astype(BF16)
        back.append(pltpu.make_async_copy(out.at[:, :, c], out_ref.at[:, :, c], outs.at[n]))
        back[-1].start()
    for copy in back:
        copy.wait()


def terms_kernel(n, xo_ref, xp_ref, do_ref, dp_ref, ho_ref, hp_ref, *refs):
    out_refs, (xo, xp, do, dp, ho, hp, out, ins, outs) = refs[1:6], refs[6:]
    size = xo.shape[0]
    rows = slice(n * size, (n + 1) * size)
    pairs = [
        (xo_ref.at[rows], xo),
        (ho_ref.at[0], ho.at[0]),
        (xp_ref.at[rows], xp),
        (hp_ref.at[0], hp.at[0]),
        (ho_ref.at[1], ho.at[1]),
        (hp_ref.at[1], hp.at[1]),
        (do_ref.at[rows], do),
        (ho_ref.at[2], ho.at[2]),
        (dp_ref.at[rows], dp),
        (hp_ref.at[2], hp.at[2]),
    ]
    copies = started(pairs, ins)
    back = []
    for i, (own, peer, ready) in enumerate(((xo, xp, copies[:4]), (xo, xp, copies[4:6]), (do, dp, copies[6:]))):
        for copy in ready:
            copy.wait()
        out[i] = (dot(own[...], ho[i]) + dot(peer[...], hp[i])).astype(BF16)
        begin = 0
        for r in out_refs:
            count = r.shape[1]
            back.append(pltpu.make_async_copy(out.at[i, begin : begin + count], r.at[i], outs.at[len(back)]))
            back[-1].start()
            begin += count
    for copy in back:
        copy.wait()


def near_kernel(up_ref, down_ref, own_up_ref, own_down_ref, *refs):
    to_up_ref, to_down_ref = refs[-2:]
    half = up_ref.shape[1]
    for own_ref, got_ref, out_ref, rows in (
        (own_up_ref, up_ref, to_up_ref, slice(0, half)),
        (own_down_ref, down_ref, to_down_ref, slice(half, 2 * half)),
    ):
        out_ref[...] = own_ref[...]
        out_ref[:, rows, :] = (own_ref[:, rows, :].astype(F32) + got_ref[...].astype(F32)).astype(BF16)


def line_kernel(own_ref, from_up_ref, from_down_ref, *refs):
    line_ref = refs[-3]
    for i in range(3):
        total = own_ref[i].astype(F32) + from_up_ref[i].astype(F32) + from_down_ref[i].astype(F32)
        line_ref[i] = total.astype(BF16)
    near_kernel(*refs[:4], *refs[-2:])


def sum_kernel(*refs):
    *in_refs, gate_ref, up_ref, down_ref = refs
    for i, out_ref in enumerate((gate_ref, up_ref, down_ref)):
        total = in_refs[0][i].astype(F32)
        for r in in_refs[1:]:
            total = total + r[i].astype(F32)
        out_ref[0] = total


def outputs_kernel(cap, hid_ref, wd_ref, wg_ref, wu_ref, out_ref, hid, wd, wg, wu, out, ins, outs):
    cuts = [slice(n * 512, (n + 1) * 512) for n in range(wd.shape[0] // 512)]
    pairs = [(hid_ref.at[2], hid.at[2]), (wd_ref.at[cuts[0]], wd.at[cuts[0]])]
    pairs += [(hid_ref.at[0:2], hid.at[0:2])]
    pairs += [(wg_ref.at[cuts[0]], wg.at[cuts[0]]), (wu_ref.at[cuts[0]], wu.at[cuts[0]])]
    for c in cuts[1:]:
        pairs += [(a.at[c], b.at[c]) for a, b in ((wd_ref, wd), (wg_ref, wg), (wu_ref, wu))]
    copies = started(pairs, ins)
    back = []
    for n, c in enumerate(cuts):
        first = copies[:2] if n == 0 else copies[3 * n + 2 : 3 * n + 3]
        then = copies[2:5] if n == 0 else copies[3 * n + 3 : 3 * n + 5]
        for copy in first:
            copy.wait()
        term = dot(hid[2], wd[c], NT).astype(BF16)
        for s in range(Y * Z):
            out[s, 0, :, c] = term[s * cap : (s + 1) * cap, :]
        for copy in then:
            copy.wait()
        term = (dot(hid[0], wg[c], NT) + dot(hid[1], wu[c], NT)).astype(BF16)
        for s in range(Y * Z):
            out[s, 1, :, c] = term[s * cap : (s + 1) * cap, :]
        back.append(pltpu.make_async_copy(out.at[:, :, :, c], out_ref.at[:, :, :, c], outs.at[n]))
        back[-1].start()
    for copy in back:
        copy.wait()


def combine_kernel(routes_ref, gates_ref, cot_ref, rows_ref, out_ref, part_ref, grad_ref):
    cap = rows_ref.shape[2]
    first, second, slot = places(routes_ref, Y * Z)
    outs = jnp.concatenate([rows_ref[e, 0] for e in range(Y * Z)], axis=0)
    parts = jnp.concatenate([rows_ref[e, 1] for e in range(Y * Z)], axis=0)
    cot = cot_ref[...].astype(F32)
    total, columns = None, []
    for k, mask in enumerate((first, second)):
        mine = dot(pick(mask, slot, cap).astype(BF16), outs, TN)
        columns.append(jnp.sum(cot * mine, axis=1, keepdims=True))
        term = gates_ref[:, k : k + 1] * mine
        total = term if total is None else total + term
    out_ref[...] = total.astype(BF16)
    part_ref[...] = dot(pick(first + second, slot, cap).astype(BF16), parts, TN).astype(BF16)
    grad_ref[...] = jnp.concatenate(columns, axis=1)


def shards(checkpoint, cotangent, routes, gates, w_gate, w_up, w_down):
    tokens, features = cotangent.shape
    dp = lax.axis_size("dp")
    ff = w_gate.shape[2]
    experts = Y * Z
    cap = tokens * routes.shape[1] * 2 // experts
    rows = experts * cap
    w_gate, w_up, w_down = w_gate[0], w_up[0], w_down[0]
    mm = 2 * rows * features * ff
    y, z = lax.axis_index("ep") // Z, lax.axis_index("ep") % Z
    mine = lax.axis_index("dp")
    line, x_at, core = mine // (X * C), mine // C % X, mine % C
    step = jnp.arange(C * L * X, dtype=jnp.int32)
    block_at = (line ^ (1 - step // X % L)) * X + (x_at + step) % X
    start = (block_at * C + (core ^ (step // (L * X)))).astype(jnp.int32) * (features // dp)
    piece_at = ((y - step[: Y * Z]) % Y * Z + (z ^ (step[: Y * Z] // Y))).astype(jnp.int32)

    routes_t, gates_t = routes.T, gates.T
    at = jnp.stack([y, z]).astype(jnp.int32)
    code_o, wide, slices, *packed = call(
        functools.partial(own_kernel, cap),
        [
            struct(2, tokens, dtype=jnp.int32),
            struct(tokens, features + tokens),
            struct(*checkpoint.shape),
            *[struct(cap, features)] * Y,
        ],
        [at, routes_t, gates_t, cotangent, checkpoint],
        2 * Y * cap * tokens * features,
        in_specs=[SMEM] + [None] * 4,
        vmem=56,
        blocks=True,
    )
    wide = lax.ppermute(wide, "ep", EP_SWAP)
    slices = lax.all_to_all(
        slices.reshape(dp, tokens, features // dp), "dp", split_axis=0, concat_axis=0, tiled=True
    )

    def to_experts(packed):
        return [packed[0]] + [lax.ppermute(packed[k], "ep", y_shift(k)) for k in range(1, Y)]

    d_own = to_experts(packed)
    (slices,) = call(copy_kernel, [struct(*slices.shape)], [slices, d_own[1]], in_specs=[None, ANY], vmem=16)
    slices_p = lax.ppermute(slices, "ep", EP_SWAP)
    code_p, *packed = call(
        functools.partial(partner_kernel, cap),
        [struct(2, tokens, dtype=jnp.int32), *[struct(cap, features)] * Y],
        [at, wide],
        2 * Y * cap * tokens * features,
        in_specs=[SMEM, None],
        vmem=16,
    )
    d_pieces = d_own + to_experts(packed)
    x_pieces = to_experts(
        call(
            functools.partial(pack_x_kernel, cap),
            [struct(2 * cap, features)] * Y,
            [code_o, code_p, slices, slices_p, d_pieces[Y]],
            4 * Y * cap * tokens * features,
            in_specs=[None] * 4 + [ANY],
            vmem=16,
        )
    )

    weight = ((features, ff), BF16)
    turned = struct(features // C, rows)
    scratch = [((rows, features), BF16), weight, ((rows, ff), F32), *[(turned.shape, BF16)] * 2]
    hidden_grad, d_own, d_other = streamed(
        hidden_grad_kernel,
        [struct(rows, ff, dtype=F32), turned, turned],
        [piece_at, start, *d_pieces, w_down],
        mm,
        scratch,
        experts + 2,
        4,
        in_specs=[SMEM] * 2 + [ANY] * (experts + 1),
    )
    d_turned = d_own, lax.ppermute(d_other, "dp", DP_SWAP_C)
    hid, x_own, x_other = streamed(
        hidden_kernel,
        [struct(3, rows, ff), turned, turned],
        [piece_at, start, *x_pieces, w_gate, w_up, hidden_grad],
        2 * mm,
        [scratch[0], weight, weight, scratch[2], ((3, rows, ff), BF16), *scratch[3:]],
        experts + 9,
        5,
        in_specs=[SMEM] * 2 + [ANY] * (Y + 3),
    )
    hid_peer = lax.ppermute(hid, "dp", DP_SWAP_C)
    x_turned = x_own, lax.ppermute(x_other, "dp", DP_SWAP_C)
    (outs,) = streamed(
        functools.partial(outputs_kernel, cap),
        [struct(experts, 2, cap, features)],
        [hid, w_down, w_gate, w_up],
        3 * mm,
        [((3, rows, ff), BF16), weight, weight, weight, ((experts, 2, cap, features), BF16)],
        14,
        4,
    )
    back = lax.all_to_all(outs, "ep", split_axis=0, concat_axis=0, tiled=True)

    half = tokens // 2
    sizes = (tokens, tokens, half, half, tokens)

    def terms_of(n, after):
        size = X * tokens
        return streamed(
            functools.partial(terms_kernel, n),
            [struct(3, count, ff) for count in sizes],
            [*x_turned, *d_turned, hid, hid_peer, after],
            3 * mm // 2,
            [((size, rows), BF16)] * 4 + [((3, rows, ff), BF16)] * 2 + [((3, size, ff), BF16)],
            10,
            15,
        )

    def small(body, count, arrays, after=()):
        return call(
            body,
            [struct(3, tokens, ff)] * count,
            [*arrays, *after],
            in_specs=[None] * len(arrays) + [ANY] * len(after),
            vmem=24,
        )

    def shift(array, k):
        return lax.ppermute(array, "dp", x_shift(k))

    there = terms_of(0, outs)
    there_up, there_down = shift(there[2], 1), shift(there[3], -1)
    here = terms_of(1, there[0])
    here_up, here_down = shift(here[2], 1), shift(here[3], -1)
    to_up, to_down = small(near_kernel, 2, (there_up, there_down, there[1], there[4]), here[:1])
    there_up, there_down = shift(to_up, 1), shift(to_down, -1)
    other, to_up, to_down = small(
        line_kernel, 3, (there[0], there_up, there_down, here_up, here_down, here[1], here[4])
    )
    other = lax.ppermute(other, "dp", DP_SWAP_L)
    here_up, here_down = shift(to_up, 1), shift(to_down, -1)
    grads = call(
        sum_kernel, [struct(1, tokens, ff, dtype=F32)] * 3, [here[0], here_up, here_down, other], vmem=24
    )
    layer_out, grad_input, grad_gates = call(
        combine_kernel,
        [struct(tokens, features), struct(tokens, features), struct(tokens, 2, dtype=F32)],
        [routes_t, gates, cotangent, back],
        6 * rows * tokens * features,
        vmem=32,
    )
    return (layer_out, grad_input, grad_gates, *grads)


def solution(mesh):
    tok = P(("ep", "dp"), None)
    weight = P("ep", None, None)
    grad = P("ep", "dp", None)
    return jax.shard_map(
        shards,
        mesh=mesh,
        in_specs=(P("ep", "dp"), tok, tok, tok, weight, weight, weight),
        out_specs=(tok, tok, tok, grad, grad, grad),
        check_vma=False,
    )
```

```python
import functools

import jax
import jax.numpy as jnp
from jax import lax
from jax.experimental import pallas as pl
from jax.experimental.pallas import tpu as pltpu
from jax.sharding import PartitionSpec as P

F32 = jnp.float32
BF16 = jnp.bfloat16
NT = (((1,), (1,)), ((), ()))
TN = (((0,), (0,)), ((), ()))
NN = (((1,), (0,)), ((), ()))
MIB = 1 << 20

Y, Z, L, X, C = 4, 2, 2, 4, 2
EP_SWAP = [(i, i ^ 1) for i in range(Y * Z)]
DP_SWAP_L = [(i, i ^ (X * C)) for i in range(L * X * C)]
DP_SWAP_C = [(i, i ^ 1) for i in range(L * X * C)]
VMEM = pl.BlockSpec(memory_space=pltpu.VMEM)
ANY = pl.BlockSpec(memory_space=pl.ANY)
SMEM = pl.BlockSpec(memory_space=pltpu.SMEM)


def y_shift(k):
    return [(y * Z + z, (y + k) % Y * Z + z) for y in range(Y) for z in range(Z)]


def x_shift(k):
    return [
        ((line * X + x) * C + c, (line * X + (x + k) % X) * C + c)
        for line in range(L)
        for x in range(X)
        for c in range(C)
    ]


def struct(*shape, dtype=BF16):
    return jax.ShapeDtypeStruct(shape, dtype)


def dot(a, b, dims=NN):
    return lax.dot_general(a, b, dims, preferred_element_type=F32)


def spec(shape, index=None):
    zeros = (0,) * len(shape)
    return pl.BlockSpec(shape, index or (lambda *_: zeros))


def call(body, out_shape, args, flops=0, in_specs=None, out_specs=None, vmem=32, scratch=(), blocks=False):
    in_specs = in_specs or [None] * len(args)
    out_specs = out_specs or [None] * len(out_shape)

    def whole(array):
        return spec(array.shape) if blocks else VMEM

    return pl.pallas_call(
        body,
        grid=(1,) if blocks else (),
        in_specs=[s or whole(a) for s, a in zip(in_specs, args, strict=True)],
        out_specs=[s or whole(a) for s, a in zip(out_specs, out_shape, strict=True)],
        out_shape=out_shape,
        scratch_shapes=scratch,
        cost_estimate=pl.CostEstimate(
            flops=flops,
            bytes_accessed=sum(a.size * a.dtype.itemsize for a in args),
            transcendentals=0,
        ),
        compiler_params=pltpu.CompilerParams(vmem_limit_bytes=vmem * MIB),
    )(*args)


def streamed(body, out_shape, args, flops, scratch, in_count, out_count, in_specs=None):
    sems = [pltpu.SemaphoreType.DMA((in_count,)), pltpu.SemaphoreType.DMA((out_count,))]
    return call(
        body,
        out_shape,
        args,
        flops,
        in_specs=in_specs or [ANY] * len(args),
        out_specs=[ANY] * len(out_shape),
        vmem=56,
        scratch=[pltpu.VMEM(shape, dtype) for shape, dtype in scratch] + sems,
    )


def started(pairs, sems):
    copies = [pltpu.make_async_copy(a, b, sems.at[n]) for n, (a, b) in enumerate(pairs)]
    for copy in copies:
        copy.start()
    return copies


def places(code_ref, count):
    tokens = code_ref.shape[1]
    expert = lax.broadcasted_iota(jnp.int32, (count, tokens), 0)
    first = (code_ref[0:1, :] == expert).astype(F32)
    second = (code_ref[1:2, :] == expert).astype(F32)
    row = lax.broadcasted_iota(jnp.int32, (tokens, tokens), 0)
    col = lax.broadcasted_iota(jnp.int32, (tokens, tokens), 1)
    before = (row < col).astype(BF16)
    slot = dot((first + second).astype(BF16), before)
    return first, second, slot


def pick(mask, slot, cap):
    count, tokens = slot.shape
    index = lax.broadcasted_iota(jnp.int32, (cap, tokens), 0).astype(F32)
    return jnp.concatenate(
        [jnp.where(index == slot[e : e + 1, :], mask[e : e + 1, :], 0.0) for e in range(count)], axis=0
    )


def codes(routes, at_ref):
    return jnp.where((routes & 1) == at_ref[1], ((routes >> 1) - at_ref[0]) & (Y - 1), -1)


def pack_d(cap, code_ref, gates, rows, out_refs):
    first, second, slot = places(code_ref, Y)
    sel = pick(first + second, slot, cap)
    weight = gates[0:1, :] * first + gates[1:2, :] * second
    scale = jnp.concatenate(
        [
            jnp.sum(sel[e * cap : (e + 1) * cap, :] * weight[e : e + 1, :], axis=1, keepdims=True)
            for e in range(Y)
        ],
        axis=0,
    )
    picked = (dot(sel.astype(BF16), rows) * scale).astype(BF16)
    for e, out_ref in enumerate(out_refs):
        out_ref[...] = picked[e * cap : (e + 1) * cap, :]


def own_kernel(cap, at_ref, routes_ref, gates_ref, cot_ref, code_ref, wide_ref, *out_refs):
    features = cot_ref.shape[1]
    wide_ref[:, 0:features] = cot_ref[...]
    gates = gates_ref[...]
    pieces, rest = [routes_ref[...].astype(F32)], gates
    for _ in range(3):
        pieces.append(rest.astype(BF16).astype(F32))
        rest = rest - pieces[-1]
    tokens = gates.shape[1]
    columns = jnp.concatenate([*pieces, jnp.zeros((tokens - 8, tokens), F32)], axis=0)
    wide_ref[:, features:] = columns.T.astype(BF16)
    code_ref[...] = codes(routes_ref[...], at_ref)
    pack_d(cap, code_ref, gates, cot_ref[...], out_refs)


def copy_kernel(in_ref, _, out_ref):
    out_ref[...] = in_ref[...]


def partner_kernel(cap, at_ref, wide_ref, *refs):
    code_ref, *out_refs = refs[-1 - Y :]
    features = out_refs[0].shape[1]
    columns = wide_ref[:, features:].astype(F32).T
    code_ref[...] = codes(columns[0:2, :].astype(jnp.int32), at_ref)
    gates = columns[2:4, :] + columns[4:6, :] + columns[6:8, :]
    pack_d(cap, code_ref, gates, wide_ref[:, 0:features], out_refs)


def pack_x_kernel(cap, code_o_ref, code_p_ref, slices_o_ref, slices_p_ref, *refs):
    out_refs = refs[-Y:]
    width = slices_o_ref.shape[2]
    for n, (code_ref, slices_ref) in enumerate(((code_o_ref, slices_o_ref), (code_p_ref, slices_p_ref))):
        first, second, slot = places(code_ref, Y)
        sel = pick(first + second, slot, cap).astype(BF16)
        for j in range(slices_ref.shape[0]):
            picked = dot(sel, slices_ref[j]).astype(BF16)
            for k, out_ref in enumerate(out_refs):
                out_ref[n * cap : (n + 1) * cap, j * width : (j + 1) * width] = picked[k * cap : (k + 1) * cap, :]


def turn(rows, start_ref, own, other):
    width = own.shape[0] // (L * X)
    for n, out in enumerate((own, other)):
        for j in range(L * X):
            begin = pl.multiple_of(start_ref[n * L * X + j], width)
            out[j * width : (j + 1) * width, :] = rows[:, pl.ds(begin, width)].T


def hidden_grad_kernel(at_ref, start_ref, *refs):
    *d_refs, w_ref, out_ref, own_ref, other_ref, d, w, out, own, other, ins, outs = refs
    cap = d_refs[0].shape[0]
    cuts = [slice(0, 512), slice(512, 1024)]
    pairs = [(r, d.at[pl.ds(pl.multiple_of(at_ref[n] * cap, cap), cap)]) for n, r in enumerate(d_refs)]
    copies = started(pairs + [(w_ref.at[:, c], w.at[:, c]) for c in cuts], ins)
    for copy in copies[: len(pairs)]:
        copy.wait()
    turn(d, start_ref, own, other)
    back = [pltpu.make_async_copy(a, b, outs.at[2 + n]) for n, (a, b) in enumerate(((own, own_ref), (other, other_ref)))]
    for copy in back:
        copy.start()
    for n, c in enumerate(cuts):
        copies[len(pairs) + n].wait()
        out[:, c] = dot(d[...], w[:, c])
        back.append(pltpu.make_async_copy(out.at[:, c], out_ref.at[:, c], outs.at[n]))
        back[-1].start()
    for copy in back:
        copy.wait()


def hidden_kernel(at_ref, start_ref, *refs):
    x_refs, refs = refs[:Y], refs[Y:]
    wg_ref, wu_ref, hg_ref, out_ref, own_ref, other_ref, x, wg, wu, hg, out, own, other, ins, outs = refs
    cuts = [slice(0, 256), slice(256, 512), slice(512, 1024)]
    cap = x_refs[0].shape[0] // 2
    pairs = [
        (r.at[n * cap : (n + 1) * cap], x.at[pl.ds(pl.multiple_of(at_ref[n * Y + k] * cap, cap), cap)])
        for k, r in enumerate(x_refs)
        for n in range(2)
    ]
    count = len(pairs)
    for c in cuts:
        pairs += [(a.at[:, c], b.at[:, c]) for a, b in ((wg_ref, wg), (wu_ref, wu), (hg_ref, hg))]
    copies = started(pairs, ins)
    for copy in copies[:count]:
        copy.wait()
    back = []
    for n, c in enumerate(cuts):
        for copy in copies[count + 3 * n : count + 3 * n + 3]:
            copy.wait()
        pre_gate = dot(x[...], wg[:, c])
        pre_up = dot(x[...], wu[:, c])
        if n == 0:
            turn(x, start_ref, own, other)
            back += [pltpu.make_async_copy(own, own_ref, outs.at[3]), pltpu.make_async_copy(other, other_ref, outs.at[4])]
            for copy in back:
                copy.start()
        hidden_grad = hg[:, c]
        s = 0.5 * jnp.tanh(0.5 * pre_gate) + 0.5
        silu = pre_gate * s
        out[0, :, c] = (hidden_grad * pre_up * s * (1.0 + pre_gate * (1.0 - s))).astype(BF16)
        out[1, :, c] = (hidden_grad * silu).astype(BF16)
        out[2, :, c] = (silu * pre_up).astype(BF16)
        back.append(pltpu.make_async_copy(out.at[:, :, c], out_ref.at[:, :, c], outs.at[n]))
        back[-1].start()
    for copy in back:
        copy.wait()


def terms_kernel(n, xo_ref, xp_ref, do_ref, dp_ref, ho_ref, hp_ref, *refs):
    out_refs, (xo, xp, do, dp, ho, hp, out, ins, outs) = refs[1:6], refs[6:]
    size = xo.shape[0]
    rows = slice(n * size, (n + 1) * size)
    pairs = [
        (xo_ref.at[rows], xo),
        (ho_ref.at[0], ho.at[0]),
        (xp_ref.at[rows], xp),
        (hp_ref.at[0], hp.at[0]),
        (ho_ref.at[1], ho.at[1]),
        (hp_ref.at[1], hp.at[1]),
        (do_ref.at[rows], do),
        (ho_ref.at[2], ho.at[2]),
        (dp_ref.at[rows], dp),
        (hp_ref.at[2], hp.at[2]),
    ]
    copies = started(pairs, ins)
    back = []
    for i, (own, peer, ready) in enumerate(((xo, xp, copies[:4]), (xo, xp, copies[4:6]), (do, dp, copies[6:]))):
        for copy in ready:
            copy.wait()
        out[i] = (dot(own[...], ho[i]) + dot(peer[...], hp[i])).astype(BF16)
        begin = 0
        for r in out_refs:
            count = r.shape[1]
            back.append(pltpu.make_async_copy(out.at[i, begin : begin + count], r.at[i], outs.at[len(back)]))
            back[-1].start()
            begin += count
    for copy in back:
        copy.wait()


def near_kernel(up_ref, down_ref, own_up_ref, own_down_ref, *refs):
    to_up_ref, to_down_ref = refs[-2:]
    half = up_ref.shape[1]
    for own_ref, got_ref, out_ref, rows in (
        (own_up_ref, up_ref, to_up_ref, slice(0, half)),
        (own_down_ref, down_ref, to_down_ref, slice(half, 2 * half)),
    ):
        out_ref[...] = own_ref[...]
        out_ref[:, rows, :] = (own_ref[:, rows, :].astype(F32) + got_ref[...].astype(F32)).astype(BF16)


def line_kernel(own_ref, from_up_ref, from_down_ref, *refs):
    line_ref = refs[-3]
    for i in range(3):
        total = own_ref[i].astype(F32) + from_up_ref[i].astype(F32) + from_down_ref[i].astype(F32)
        line_ref[i] = total.astype(BF16)
    near_kernel(*refs[:4], *refs[-2:])


def sum_kernel(*refs):
    *in_refs, gate_ref, up_ref, down_ref = refs
    for i, out_ref in enumerate((gate_ref, up_ref, down_ref)):
        total = in_refs[0][i].astype(F32)
        for r in in_refs[1:]:
            total = total + r[i].astype(F32)
        out_ref[0] = total


def outputs_kernel(cap, hid_ref, wd_ref, wg_ref, wu_ref, out_ref, hid, wd, wg, wu, out, ins, outs):
    cuts = [slice(n * 512, (n + 1) * 512) for n in range(wd.shape[0] // 512)]
    pairs = [(hid_ref.at[2], hid.at[2]), (wd_ref.at[cuts[0]], wd.at[cuts[0]])]
    pairs += [(hid_ref.at[0:2], hid.at[0:2])]
    pairs += [(wg_ref.at[cuts[0]], wg.at[cuts[0]]), (wu_ref.at[cuts[0]], wu.at[cuts[0]])]
    for c in cuts[1:]:
        pairs += [(a.at[c], b.at[c]) for a, b in ((wd_ref, wd), (wg_ref, wg), (wu_ref, wu))]
    copies = started(pairs, ins)
    back = []
    for n, c in enumerate(cuts):
        first = copies[:2] if n == 0 else copies[3 * n + 2 : 3 * n + 3]
        then = copies[2:5] if n == 0 else copies[3 * n + 3 : 3 * n + 5]
        for copy in first:
            copy.wait()
        term = dot(hid[2], wd[c], NT).astype(BF16)
        for s in range(Y * Z):
            out[s, 0, :, c] = term[s * cap : (s + 1) * cap, :]
        for copy in then:
            copy.wait()
        term = (dot(hid[0], wg[c], NT) + dot(hid[1], wu[c], NT)).astype(BF16)
        for s in range(Y * Z):
            out[s, 1, :, c] = term[s * cap : (s + 1) * cap, :]
        back.append(pltpu.make_async_copy(out.at[:, :, :, c], out_ref.at[:, :, :, c], outs.at[n]))
        back[-1].start()
    for copy in back:
        copy.wait()


def combine_kernel(routes_ref, gates_ref, cot_ref, rows_ref, out_ref, part_ref, grad_ref):
    cap = rows_ref.shape[2]
    first, second, slot = places(routes_ref, Y * Z)
    outs = jnp.concatenate([rows_ref[e, 0] for e in range(Y * Z)], axis=0)
    parts = jnp.concatenate([rows_ref[e, 1] for e in range(Y * Z)], axis=0)
    cot = cot_ref[...].astype(F32)
    total, columns = None, []
    for k, mask in enumerate((first, second)):
        mine = dot(pick(mask, slot, cap).astype(BF16), outs, TN)
        columns.append(jnp.sum(cot * mine, axis=1, keepdims=True))
        term = gates_ref[:, k : k + 1] * mine
        total = term if total is None else total + term
    out_ref[...] = total.astype(BF16)
    part_ref[...] = dot(pick(first + second, slot, cap).astype(BF16), parts, TN).astype(BF16)
    grad_ref[...] = jnp.concatenate(columns, axis=1)


def shards(checkpoint, cotangent, routes, gates, w_gate, w_up, w_down):
    tokens, features = cotangent.shape
    dp = lax.axis_size("dp")
    ff = w_gate.shape[2]
    experts = Y * Z
    cap = tokens * routes.shape[1] * 2 // experts
    rows = experts * cap
    w_gate, w_up, w_down = w_gate[0], w_up[0], w_down[0]
    mm = 2 * rows * features * ff
    y, z = lax.axis_index("ep") // Z, lax.axis_index("ep") % Z
    mine = lax.axis_index("dp")
    line, x_at, core = mine // (X * C), mine // C % X, mine % C
    step = jnp.arange(C * L * X, dtype=jnp.int32)
    block_at = (line ^ (1 - step // X % L)) * X + (x_at + step) % X
    start = (block_at * C + (core ^ (step // (L * X)))).astype(jnp.int32) * (features // dp)
    piece_at = ((y - step[: Y * Z]) % Y * Z + (z ^ (step[: Y * Z] // Y))).astype(jnp.int32)

    routes_t, gates_t = routes.T, gates.T
    at = jnp.stack([y, z]).astype(jnp.int32)
    code_o, wide, *packed = call(
        functools.partial(own_kernel, cap),
        [
            struct(2, tokens, dtype=jnp.int32),
            struct(tokens, features + tokens),
            *[struct(cap, features)] * Y,
        ],
        [at, routes_t, gates_t, cotangent],
        2 * Y * cap * tokens * features,
        in_specs=[SMEM] + [None] * 3,
        vmem=56,
        blocks=True,
    )
    wide = lax.ppermute(wide, "ep", EP_SWAP)
    slices = lax.all_to_all(
        checkpoint.reshape(dp, tokens, features // dp), "dp", split_axis=0, concat_axis=0, tiled=True
    )

    def to_experts(packed):
        return [packed[0]] + [lax.ppermute(packed[k], "ep", y_shift(k)) for k in range(1, Y)]

    d_own = to_experts(packed)
    (slices,) = call(copy_kernel, [struct(*slices.shape)], [slices, d_own[1]], in_specs=[None, ANY], vmem=16)
    slices_p = lax.ppermute(slices, "ep", EP_SWAP)
    code_p, *packed = call(
        functools.partial(partner_kernel, cap),
        [struct(2, tokens, dtype=jnp.int32), *[struct(cap, features)] * Y],
        [at, wide],
        2 * Y * cap * tokens * features,
        in_specs=[SMEM, None],
        vmem=16,
    )
    d_pieces = d_own + to_experts(packed)
    x_pieces = to_experts(
        call(
            functools.partial(pack_x_kernel, cap),
            [struct(2 * cap, features)] * Y,
            [code_o, code_p, slices, slices_p, d_pieces[Y]],
            4 * Y * cap * tokens * features,
            in_specs=[None] * 4 + [ANY],
            vmem=16,
        )
    )

    weight = ((features, ff), BF16)
    turned = struct(features // C, rows)
    scratch = [((rows, features), BF16), weight, ((rows, ff), F32), *[(turned.shape, BF16)] * 2]
    hidden_grad, d_own, d_other = streamed(
        hidden_grad_kernel,
        [struct(rows, ff, dtype=F32), turned, turned],
        [piece_at, start, *d_pieces, w_down],
        mm,
        scratch,
        experts + 2,
        4,
        in_specs=[SMEM] * 2 + [ANY] * (experts + 1),
    )
    d_turned = d_own, lax.ppermute(d_other, "dp", DP_SWAP_C)
    hid, x_own, x_other = streamed(
        hidden_kernel,
        [struct(3, rows, ff), turned, turned],
        [piece_at, start, *x_pieces, w_gate, w_up, hidden_grad],
        2 * mm,
        [scratch[0], weight, weight, scratch[2], ((3, rows, ff), BF16), *scratch[3:]],
        experts + 9,
        5,
        in_specs=[SMEM] * 2 + [ANY] * (Y + 3),
    )
    hid_peer = lax.ppermute(hid, "dp", DP_SWAP_C)
    x_turned = x_own, lax.ppermute(x_other, "dp", DP_SWAP_C)
    (outs,) = streamed(
        functools.partial(outputs_kernel, cap),
        [struct(experts, 2, cap, features)],
        [hid, w_down, w_gate, w_up],
        3 * mm,
        [((3, rows, ff), BF16), weight, weight, weight, ((experts, 2, cap, features), BF16)],
        14,
        4,
    )
    back = lax.all_to_all(outs, "ep", split_axis=0, concat_axis=0, tiled=True)

    half = tokens // 2
    sizes = (tokens, tokens, half, half, tokens)

    def terms_of(n, after):
        size = X * tokens
        return streamed(
            functools.partial(terms_kernel, n),
            [struct(3, count, ff) for count in sizes],
            [*x_turned, *d_turned, hid, hid_peer, after],
            3 * mm // 2,
            [((size, rows), BF16)] * 4 + [((3, rows, ff), BF16)] * 2 + [((3, size, ff), BF16)],
            10,
            15,
        )

    def small(body, count, arrays, after=()):
        return call(
            body,
            [struct(3, tokens, ff)] * count,
            [*arrays, *after],
            in_specs=[None] * len(arrays) + [ANY] * len(after),
            vmem=24,
        )

    def shift(array, k):
        return lax.ppermute(array, "dp", x_shift(k))

    there = terms_of(0, outs)
    there_up, there_down = shift(there[2], 1), shift(there[3], -1)
    here = terms_of(1, there[0])
    here_up, here_down = shift(here[2], 1), shift(here[3], -1)
    to_up, to_down = small(near_kernel, 2, (there_up, there_down, there[1], there[4]), here[:1])
    there_up, there_down = shift(to_up, 1), shift(to_down, -1)
    other, to_up, to_down = small(
        line_kernel, 3, (there[0], there_up, there_down, here_up, here_down, here[1], here[4])
    )
    other = lax.ppermute(other, "dp", DP_SWAP_L)
    here_up, here_down = shift(to_up, 1), shift(to_down, -1)
    grads = call(
        sum_kernel, [struct(1, tokens, ff, dtype=F32)] * 3, [here[0], here_up, here_down, other], vmem=24
    )
    layer_out, grad_input, grad_gates = call(
        combine_kernel,
        [struct(tokens, features), struct(tokens, features), struct(tokens, 2, dtype=F32)],
        [routes_t, gates, cotangent, back],
        6 * rows * tokens * features,
        vmem=32,
    )
    return (layer_out, grad_input, grad_gates, *grads)


def solution(mesh):
    tok = P(("ep", "dp"), None)
    weight = P("ep", None, None)
    grad = P("ep", "dp", None)
    return jax.shard_map(
        shards,
        mesh=mesh,
        in_specs=(P("ep", "dp"), tok, tok, tok, weight, weight, weight),
        out_specs=(tok, tok, tok, grad, grad, grad),
        check_vma=False,
    )
```

```python
import functools

import jax
import jax.numpy as jnp
from jax import lax
from jax.experimental import pallas as pl
from jax.experimental.pallas import tpu as pltpu
from jax.sharding import PartitionSpec as P

F32 = jnp.float32
BF16 = jnp.bfloat16
NT = (((1,), (1,)), ((), ()))
TN = (((0,), (0,)), ((), ()))
NN = (((1,), (0,)), ((), ()))
MIB = 1 << 20

Y, Z, L, X, C = 4, 2, 2, 4, 2
EP_SWAP = [(i, i ^ 1) for i in range(Y * Z)]
DP_SWAP_L = [(i, i ^ (X * C)) for i in range(L * X * C)]
DP_SWAP_C = [(i, i ^ 1) for i in range(L * X * C)]
VMEM = pl.BlockSpec(memory_space=pltpu.VMEM)
ANY = pl.BlockSpec(memory_space=pl.ANY)
SMEM = pl.BlockSpec(memory_space=pltpu.SMEM)


def y_shift(k):
    return [(y * Z + z, (y + k) % Y * Z + z) for y in range(Y) for z in range(Z)]


def x_shift(k):
    return [
        ((line * X + x) * C + c, (line * X + (x + k) % X) * C + c)
        for line in range(L)
        for x in range(X)
        for c in range(C)
    ]


def struct(*shape, dtype=BF16):
    return jax.ShapeDtypeStruct(shape, dtype)


def dot(a, b, dims=NN):
    return lax.dot_general(a, b, dims, preferred_element_type=F32)


def spec(shape, index=None):
    zeros = (0,) * len(shape)
    return pl.BlockSpec(shape, index or (lambda *_: zeros))


def call(body, out_shape, args, flops=0, in_specs=None, out_specs=None, vmem=32, scratch=(), blocks=False):
    in_specs = in_specs or [None] * len(args)
    out_specs = out_specs or [None] * len(out_shape)

    def whole(array):
        return spec(array.shape) if blocks else VMEM

    return pl.pallas_call(
        body,
        grid=(1,) if blocks else (),
        in_specs=[s or whole(a) for s, a in zip(in_specs, args, strict=True)],
        out_specs=[s or whole(a) for s, a in zip(out_specs, out_shape, strict=True)],
        out_shape=out_shape,
        scratch_shapes=scratch,
        cost_estimate=pl.CostEstimate(
            flops=flops,
            bytes_accessed=sum(a.size * a.dtype.itemsize for a in args),
            transcendentals=0,
        ),
        compiler_params=pltpu.CompilerParams(vmem_limit_bytes=vmem * MIB),
    )(*args)


def streamed(body, out_shape, args, flops, scratch, in_count, out_count, in_specs=None):
    sems = [pltpu.SemaphoreType.DMA((in_count,)), pltpu.SemaphoreType.DMA((out_count,))]
    return call(
        body,
        out_shape,
        args,
        flops,
        in_specs=in_specs or [ANY] * len(args),
        out_specs=[ANY] * len(out_shape),
        vmem=56,
        scratch=[pltpu.VMEM(shape, dtype) for shape, dtype in scratch] + sems,
    )


def started(pairs, sems):
    copies = [pltpu.make_async_copy(a, b, sems.at[n]) for n, (a, b) in enumerate(pairs)]
    for copy in copies:
        copy.start()
    return copies


def places(code_ref, count):
    tokens = code_ref.shape[1]
    expert = lax.broadcasted_iota(jnp.int32, (count, tokens), 0)
    first = (code_ref[0:1, :] == expert).astype(F32)
    second = (code_ref[1:2, :] == expert).astype(F32)
    row = lax.broadcasted_iota(jnp.int32, (tokens, tokens), 0)
    col = lax.broadcasted_iota(jnp.int32, (tokens, tokens), 1)
    before = (row < col).astype(BF16)
    slot = dot((first + second).astype(BF16), before)
    return first, second, slot


def pick(mask, slot, cap):
    count, tokens = slot.shape
    index = lax.broadcasted_iota(jnp.int32, (cap, tokens), 0).astype(F32)
    return jnp.concatenate(
        [jnp.where(index == slot[e : e + 1, :], mask[e : e + 1, :], 0.0) for e in range(count)], axis=0
    )


def codes(routes, at_ref):
    return jnp.where((routes & 1) == at_ref[1], ((routes >> 1) - at_ref[0]) & (Y - 1), -1)


def pack_d(cap, code_ref, gates, rows, out_refs):
    first, second, slot = places(code_ref, Y)
    sel = pick(first + second, slot, cap)
    weight = gates[0:1, :] * first + gates[1:2, :] * second
    scale = jnp.concatenate(
        [
            jnp.sum(sel[e * cap : (e + 1) * cap, :] * weight[e : e + 1, :], axis=1, keepdims=True)
            for e in range(Y)
        ],
        axis=0,
    )
    picked = (dot(sel.astype(BF16), rows) * scale).astype(BF16)
    for e, out_ref in enumerate(out_refs):
        out_ref[...] = picked[e * cap : (e + 1) * cap, :]


def own_kernel(cap, at_ref, routes_ref, gates_ref, cot_ref, code_ref, wide_ref, *out_refs):
    features = cot_ref.shape[1]
    wide_ref[:, 0:features] = cot_ref[...]
    gates = gates_ref[...]
    pieces, rest = [routes_ref[...].astype(F32)], gates
    for _ in range(3):
        pieces.append(rest.astype(BF16).astype(F32))
        rest = rest - pieces[-1]
    tokens = gates.shape[1]
    columns = jnp.concatenate([*pieces, jnp.zeros((tokens - 8, tokens), F32)], axis=0)
    wide_ref[:, features:] = columns.T.astype(BF16)
    code_ref[...] = codes(routes_ref[...], at_ref)
    pack_d(cap, code_ref, gates, cot_ref[...], out_refs)


def copy_kernel(in_ref, _, out_ref):
    out_ref[...] = in_ref[...]


def partner_kernel(cap, at_ref, wide_ref, *refs):
    code_ref, *out_refs = refs[-1 - Y :]
    features = out_refs[0].shape[1]
    columns = wide_ref[:, features:].astype(F32).T
    code_ref[...] = codes(columns[0:2, :].astype(jnp.int32), at_ref)
    gates = columns[2:4, :] + columns[4:6, :] + columns[6:8, :]
    pack_d(cap, code_ref, gates, wide_ref[:, 0:features], out_refs)


def pack_x_kernel(cap, code_o_ref, code_p_ref, slices_o_ref, slices_p_ref, *refs):
    out_refs = refs[-Y:]
    width = slices_o_ref.shape[2]
    for n, (code_ref, slices_ref) in enumerate(((code_o_ref, slices_o_ref), (code_p_ref, slices_p_ref))):
        first, second, slot = places(code_ref, Y)
        sel = pick(first + second, slot, cap).astype(BF16)
        for j in range(slices_ref.shape[0]):
            picked = dot(sel, slices_ref[j]).astype(BF16)
            for k, out_ref in enumerate(out_refs):
                out_ref[n * cap : (n + 1) * cap, j * width : (j + 1) * width] = picked[k * cap : (k + 1) * cap, :]


def turn(rows, start_ref, own, other):
    width = own.shape[0] // (L * X)
    for n, out in enumerate((own, other)):
        for j in range(L * X):
            begin = pl.multiple_of(start_ref[n * L * X + j], width)
            out[j * width : (j + 1) * width, :] = rows[:, pl.ds(begin, width)].T


def hidden_grad_kernel(at_ref, start_ref, *refs):
    *d_refs, w_ref, out_ref, own_ref, other_ref, d, w, out, own, other, ins, outs = refs
    cap = d_refs[0].shape[0]
    cuts = [slice(0, 512), slice(512, 1024)]
    pairs = [(r, d.at[pl.ds(pl.multiple_of(at_ref[n] * cap, cap), cap)]) for n, r in enumerate(d_refs)]
    copies = started(pairs + [(w_ref.at[:, c], w.at[:, c]) for c in cuts], ins)
    for copy in copies[: len(pairs)]:
        copy.wait()
    turn(d, start_ref, own, other)
    back = [pltpu.make_async_copy(a, b, outs.at[2 + n]) for n, (a, b) in enumerate(((own, own_ref), (other, other_ref)))]
    for copy in back:
        copy.start()
    for n, c in enumerate(cuts):
        copies[len(pairs) + n].wait()
        out[:, c] = dot(d[...], w[:, c])
        back.append(pltpu.make_async_copy(out.at[:, c], out_ref.at[:, c], outs.at[n]))
        back[-1].start()
    for copy in back:
        copy.wait()


def hidden_kernel(at_ref, start_ref, *refs):
    x_refs, refs = refs[:Y], refs[Y:]
    wg_ref, wu_ref, hg_ref, out_ref, own_ref, other_ref, x, wg, wu, hg, out, own, other, ins, outs = refs
    cuts = [slice(0, 512), slice(512, 1024)]
    cap = x_refs[0].shape[0] // 2
    pairs = [
        (r.at[n * cap : (n + 1) * cap], x.at[pl.ds(pl.multiple_of(at_ref[n * Y + k] * cap, cap), cap)])
        for k, r in enumerate(x_refs)
        for n in range(2)
    ]
    count = len(pairs)
    for c in cuts:
        pairs += [(a.at[:, c], b.at[:, c]) for a, b in ((wg_ref, wg), (wu_ref, wu), (hg_ref, hg))]
    copies = started(pairs, ins)
    for copy in copies[:count]:
        copy.wait()
    back = []
    for n, c in enumerate(cuts):
        for copy in copies[count + 3 * n : count + 3 * n + 3]:
            copy.wait()
        pre_gate = dot(x[...], wg[:, c])
        pre_up = dot(x[...], wu[:, c])
        if n == 0:
            turn(x, start_ref, own, other)
            back += [pltpu.make_async_copy(own, own_ref, outs.at[3]), pltpu.make_async_copy(other, other_ref, outs.at[4])]
            for copy in back:
                copy.start()
        hidden_grad = hg[:, c]
        s = 0.5 * jnp.tanh(0.5 * pre_gate) + 0.5
        silu = pre_gate * s
        out[0, :, c] = (hidden_grad * pre_up * s * (1.0 + pre_gate * (1.0 - s))).astype(BF16)
        out[1, :, c] = (hidden_grad * silu).astype(BF16)
        out[2, :, c] = (silu * pre_up).astype(BF16)
        back.append(pltpu.make_async_copy(out.at[:, :, c], out_ref.at[:, :, c], outs.at[n]))
        back[-1].start()
    for copy in back:
        copy.wait()


def terms_kernel(n, xo_ref, xp_ref, do_ref, dp_ref, ho_ref, hp_ref, *refs):
    out_refs, (xo, xp, do, dp, ho, hp, out, ins, outs) = refs[1:6], refs[6:]
    size = xo.shape[0]
    rows = slice(n * size, (n + 1) * size)
    pairs = [
        (xo_ref.at[rows], xo),
        (ho_ref.at[0], ho.at[0]),
        (xp_ref.at[rows], xp),
        (hp_ref.at[0], hp.at[0]),
        (ho_ref.at[1], ho.at[1]),
        (hp_ref.at[1], hp.at[1]),
        (do_ref.at[rows], do),
        (ho_ref.at[2], ho.at[2]),
        (dp_ref.at[rows], dp),
        (hp_ref.at[2], hp.at[2]),
    ]
    copies = started(pairs, ins)
    back = []
    for i, (own, peer, ready) in enumerate(((xo, xp, copies[:4]), (xo, xp, copies[4:6]), (do, dp, copies[6:]))):
        for copy in ready:
            copy.wait()
        out[i] = (dot(own[...], ho[i]) + dot(peer[...], hp[i])).astype(BF16)
        begin = 0
        for r in out_refs:
            count = r.shape[1]
            back.append(pltpu.make_async_copy(out.at[i, begin : begin + count], r.at[i], outs.at[len(back)]))
            back[-1].start()
            begin += count
    for copy in back:
        copy.wait()


def near_kernel(up_ref, down_ref, own_up_ref, own_down_ref, *refs):
    to_up_ref, to_down_ref = refs[-2:]
    half = up_ref.shape[1]
    for own_ref, got_ref, out_ref, rows in (
        (own_up_ref, up_ref, to_up_ref, slice(0, half)),
        (own_down_ref, down_ref, to_down_ref, slice(half, 2 * half)),
    ):
        out_ref[...] = own_ref[...]
        out_ref[:, rows, :] = (own_ref[:, rows, :].astype(F32) + got_ref[...].astype(F32)).astype(BF16)


def line_kernel(own_ref, from_up_ref, from_down_ref, *refs):
    line_ref = refs[-3]
    for i in range(3):
        total = own_ref[i].astype(F32) + from_up_ref[i].astype(F32) + from_down_ref[i].astype(F32)
        line_ref[i] = total.astype(BF16)
    near_kernel(*refs[:4], *refs[-2:])


def sum_kernel(*refs):
    *in_refs, gate_ref, up_ref, down_ref = refs
    for i, out_ref in enumerate((gate_ref, up_ref, down_ref)):
        total = in_refs[0][i].astype(F32)
        for r in in_refs[1:]:
            total = total + r[i].astype(F32)
        out_ref[0] = total


def outputs_kernel(cap, hid_ref, wd_ref, wg_ref, wu_ref, out_ref, hid, wd, wg, wu, out, ins, outs):
    cuts = [slice(n * 1024, (n + 1) * 1024) for n in range(wd.shape[0] // 1024)]
    pairs = [(hid_ref.at[2], hid.at[2]), (wd_ref.at[cuts[0]], wd.at[cuts[0]])]
    pairs += [(hid_ref.at[0:2], hid.at[0:2])]
    pairs += [(wg_ref.at[cuts[0]], wg.at[cuts[0]]), (wu_ref.at[cuts[0]], wu.at[cuts[0]])]
    for c in cuts[1:]:
        pairs += [(a.at[c], b.at[c]) for a, b in ((wd_ref, wd), (wg_ref, wg), (wu_ref, wu))]
    copies = started(pairs, ins)
    back = []
    for n, c in enumerate(cuts):
        first = copies[:2] if n == 0 else copies[3 * n + 2 : 3 * n + 3]
        then = copies[2:5] if n == 0 else copies[3 * n + 3 : 3 * n + 5]
        for copy in first:
            copy.wait()
        term = dot(hid[2], wd[c], NT).astype(BF16)
        for s in range(Y * Z):
            out[s, 0, :, c] = term[s * cap : (s + 1) * cap, :]
        for copy in then:
            copy.wait()
        term = (dot(hid[0], wg[c], NT) + dot(hid[1], wu[c], NT)).astype(BF16)
        for s in range(Y * Z):
            out[s, 1, :, c] = term[s * cap : (s + 1) * cap, :]
        back.append(pltpu.make_async_copy(out.at[:, :, :, c], out_ref.at[:, :, :, c], outs.at[n]))
        back[-1].start()
    for copy in back:
        copy.wait()


def combine_kernel(routes_ref, gates_ref, cot_ref, rows_ref, out_ref, part_ref, grad_ref):
    cap = rows_ref.shape[2]
    first, second, slot = places(routes_ref, Y * Z)
    outs = jnp.concatenate([rows_ref[e, 0] for e in range(Y * Z)], axis=0)
    parts = jnp.concatenate([rows_ref[e, 1] for e in range(Y * Z)], axis=0)
    cot = cot_ref[...].astype(F32)
    total, columns = None, []
    for k, mask in enumerate((first, second)):
        mine = dot(pick(mask, slot, cap).astype(BF16), outs, TN)
        columns.append(jnp.sum(cot * mine, axis=1, keepdims=True))
        term = gates_ref[:, k : k + 1] * mine
        total = term if total is None else total + term
    out_ref[...] = total.astype(BF16)
    part_ref[...] = dot(pick(first + second, slot, cap).astype(BF16), parts, TN).astype(BF16)
    grad_ref[...] = jnp.concatenate(columns, axis=1)


def shards(checkpoint, cotangent, routes, gates, w_gate, w_up, w_down):
    tokens, features = cotangent.shape
    dp = lax.axis_size("dp")
    ff = w_gate.shape[2]
    experts = Y * Z
    cap = tokens * routes.shape[1] * 2 // experts
    rows = experts * cap
    w_gate, w_up, w_down = w_gate[0], w_up[0], w_down[0]
    mm = 2 * rows * features * ff
    y, z = lax.axis_index("ep") // Z, lax.axis_index("ep") % Z
    mine = lax.axis_index("dp")
    line, x_at, core = mine // (X * C), mine // C % X, mine % C
    step = jnp.arange(C * L * X, dtype=jnp.int32)
    block_at = (line ^ (1 - step // X % L)) * X + (x_at + step) % X
    start = (block_at * C + (core ^ (step // (L * X)))).astype(jnp.int32) * (features // dp)
    piece_at = ((y - step[: Y * Z]) % Y * Z + (z ^ (step[: Y * Z] // Y))).astype(jnp.int32)

    routes_t, gates_t = routes.T, gates.T
    at = jnp.stack([y, z]).astype(jnp.int32)
    code_o, wide, *packed = call(
        functools.partial(own_kernel, cap),
        [
            struct(2, tokens, dtype=jnp.int32),
            struct(tokens, features + tokens),
            *[struct(cap, features)] * Y,
        ],
        [at, routes_t, gates_t, cotangent],
        2 * Y * cap * tokens * features,
        in_specs=[SMEM] + [None] * 3,
        vmem=56,
        blocks=True,
    )
    wide = lax.ppermute(wide, "ep", EP_SWAP)
    slices = lax.all_to_all(
        checkpoint.reshape(dp, tokens, features // dp), "dp", split_axis=0, concat_axis=0, tiled=True
    )

    def to_experts(packed):
        return [packed[0]] + [lax.ppermute(packed[k], "ep", y_shift(k)) for k in range(1, Y)]

    d_own = to_experts(packed)
    (slices,) = call(copy_kernel, [struct(*slices.shape)], [slices, d_own[2]], in_specs=[None, ANY], vmem=16)
    slices_p = lax.ppermute(slices, "ep", EP_SWAP)
    code_p, *packed = call(
        functools.partial(partner_kernel, cap),
        [struct(2, tokens, dtype=jnp.int32), *[struct(cap, features)] * Y],
        [at, wide],
        2 * Y * cap * tokens * features,
        in_specs=[SMEM, None],
        vmem=16,
    )
    d_pieces = d_own + to_experts(packed)
    x_pieces = to_experts(
        call(
            functools.partial(pack_x_kernel, cap),
            [struct(2 * cap, features)] * Y,
            [code_o, code_p, slices, slices_p, d_pieces[Y]],
            4 * Y * cap * tokens * features,
            in_specs=[None] * 4 + [ANY],
            vmem=16,
        )
    )

    weight = ((features, ff), BF16)
    turned = struct(features // C, rows)
    scratch = [((rows, features), BF16), weight, ((rows, ff), F32), *[(turned.shape, BF16)] * 2]
    hidden_grad, d_own, d_other = streamed(
        hidden_grad_kernel,
        [struct(rows, ff, dtype=F32), turned, turned],
        [piece_at, start, *d_pieces, w_down],
        mm,
        scratch,
        experts + 2,
        4,
        in_specs=[SMEM] * 2 + [ANY] * (experts + 1),
    )
    d_turned = d_own, lax.ppermute(d_other, "dp", DP_SWAP_C)
    hid, x_own, x_other = streamed(
        hidden_kernel,
        [struct(3, rows, ff), turned, turned],
        [piece_at, start, *x_pieces, w_gate, w_up, hidden_grad],
        2 * mm,
        [scratch[0], weight, weight, scratch[2], ((3, rows, ff), BF16), *scratch[3:]],
        experts + 9,
        5,
        in_specs=[SMEM] * 2 + [ANY] * (Y + 3),
    )
    hid_peer = lax.ppermute(hid, "dp", DP_SWAP_C)
    x_turned = x_own, lax.ppermute(x_other, "dp", DP_SWAP_C)
    (outs,) = streamed(
        functools.partial(outputs_kernel, cap),
        [struct(experts, 2, cap, features)],
        [hid, w_down, w_gate, w_up],
        3 * mm,
        [((3, rows, ff), BF16), weight, weight, weight, ((experts, 2, cap, features), BF16)],
        14,
        4,
    )
    back = lax.all_to_all(outs, "ep", split_axis=0, concat_axis=0, tiled=True)

    half = tokens // 2
    sizes = (tokens, tokens, half, half, tokens)

    def terms_of(n, after):
        size = X * tokens
        return streamed(
            functools.partial(terms_kernel, n),
            [struct(3, count, ff) for count in sizes],
            [*x_turned, *d_turned, hid, hid_peer, after],
            3 * mm // 2,
            [((size, rows), BF16)] * 4 + [((3, rows, ff), BF16)] * 2 + [((3, size, ff), BF16)],
            10,
            15,
        )

    def small(body, count, arrays, after=()):
        return call(
            body,
            [struct(3, tokens, ff)] * count,
            [*arrays, *after],
            in_specs=[None] * len(arrays) + [ANY] * len(after),
            vmem=24,
        )

    def shift(array, k):
        return lax.ppermute(array, "dp", x_shift(k))

    there = terms_of(0, outs)
    there_up, there_down = shift(there[2], 1), shift(there[3], -1)
    here = terms_of(1, there[0])
    here_up, here_down = shift(here[2], 1), shift(here[3], -1)
    to_up, to_down = small(near_kernel, 2, (there_up, there_down, there[1], there[4]), here[:1])
    there_up, there_down = shift(to_up, 1), shift(to_down, -1)
    other, to_up, to_down = small(
        line_kernel, 3, (there[0], there_up, there_down, here_up, here_down, here[1], here[4])
    )
    other = lax.ppermute(other, "dp", DP_SWAP_L)
    here_up, here_down = shift(to_up, 1), shift(to_down, -1)
    grads = call(
        sum_kernel, [struct(1, tokens, ff, dtype=F32)] * 3, [here[0], here_up, here_down, other], vmem=24
    )
    layer_out, grad_input, grad_gates = call(
        combine_kernel,
        [struct(tokens, features), struct(tokens, features), struct(tokens, 2, dtype=F32)],
        [routes_t, gates, cotangent, back],
        6 * rows * tokens * features,
        vmem=32,
    )
    return (layer_out, grad_input, grad_gates, *grads)


def solution(mesh):
    tok = P(("ep", "dp"), None)
    weight = P("ep", None, None)
    grad = P("ep", "dp", None)
    return jax.shard_map(
        shards,
        mesh=mesh,
        in_specs=(P("ep", "dp"), tok, tok, tok, weight, weight, weight),
        out_specs=(tok, tok, tok, grad, grad, grad),
        check_vma=False,
    )
```
